256 devices in a mesh: ctx: 8 (over y_lo, x), grp: 16 (over y_hi, z), head: 2 (over core).
Axes of the slice: x: 4, y: 4 (y_hi: 2, y_lo: 2; y = y_hi * 2 + y_lo), z: 8, core: 2. Of those that a mesh axis runs over, the one named last changes fastest.
Arguments:
- queries: bfloat16 [16, 4, 4, 8, 2048], P('grp', None, None, 'head', 'ctx'), may hold values from -120 to 120
- fresh_key_value: bfloat16 [16, 4, 4, 8, 256], P('grp', None, None, 'head'), may hold values from -16 to 16
- key_value_cache: bfloat16 [16, 4, 4096, 8, 256], P('grp', None, 'ctx', 'head'), may hold values from -6 to 6
- lens: int32 [16, 4], P('grp'), may hold values from 512 to 4096
- blocks: bfloat16 [16384, 16, 8, 256], P(('ctx', 'grp', 'head')), may hold values from -6 to 6
- block_group: int32 [16384, 1], P(('ctx', 'grp', 'head')), may hold values from 0 to 15; in each aligned block of 64 rows (0 to 63, 64 to 127, ...) at most 8 rows name the same one
- block_request: int32 [16384], P(('ctx', 'grp', 'head')), may hold values from 0 to 3
Outputs:
- attention: bfloat16 [16, 4, 4, 8, 2048], P('grp', None, None, 'head', 'ctx')
The draws below stay inside these ranges and needn't reach their ends.
Inputs may be any that keep to these rules, and one draw needn't show every extreme that they name: `block_group`: among the 64 blocks of one device at most 8 name the same group, a bound that some block reaches.
All inputs are finite; a program needn't handle non-finite values.
Results may differ from the reference program's by a relative error of at most 0.011.
Values may be sent and summed in bfloat16 or wider, within the bound.
No kernel may reach another device: no remote copies, remote signals or barrier semaphores. Data moves between devices by JAX's collectives and lax.ppermute only.
A program may use at most 128 MiB of HBM per device.

```python
import math
import jax
import jax.numpy as jnp
import numpy as np
from jax import lax

KEY_HEADS = 8
HEAD_WIDTH = 128
QUERY_PER_KEY = 16
DECODE_STEPS = 4
GROUP_REQUESTS = 4
SHARD_CAPACITY = 512
NB = 64
BLOCK_POSITIONS = 16
MOST = 8
TOTAL_BLOCKS = 16384
N_CTX = 8
N_GRP = 16
N_HEAD = 2


def anchor_keys(key):
    sample_draw = jax.random.normal(jax.random.fold_in(key, 91), (N_GRP, GROUP_REQUESTS, 2, KEY_HEADS, HEAD_WIDTH), jnp.float32)
    return jnp.clip(sample_draw, -4.0, 4.0)


def draw_key_value_cache(key, part):
    anchors = anchor_keys(key)
    key = jax.random.fold_in(key, 5)
    complete_shape = (N_GRP, GROUP_REQUESTS, N_CTX * SHARD_CAPACITY, KEY_HEADS, 2 * HEAD_WIDTH)
    sampled = jnp.clip(jax.random.normal(key, complete_shape, jnp.float32), -6.0, 6.0)
    second_key = anchors[:, :, 1]
    sampled = sampled.at[:, :, 0, :, :HEAD_WIDTH].set(anchors[:, :, 0])
    sampled = sampled.at[:, :, 1, :, :HEAD_WIDTH].set(second_key)
    return sampled.astype(jnp.bfloat16)


def draw_queries(key, part):
    key = jax.random.fold_in(key, 6)
    complete_shape = (N_GRP, GROUP_REQUESTS, DECODE_STEPS, KEY_HEADS, QUERY_PER_KEY * HEAD_WIDTH)
    sampled = jnp.clip(jax.random.normal(key, complete_shape, jnp.float32), -6.0, 6.0)
    return sampled.astype(jnp.bfloat16)


def touch_ends(values, key, least, largest):
    index_at = [jax.random.randint(jax.random.fold_in(key, axis), (), 0, length) for axis, length in enumerate(values.shape)]
    main_axis = values.shape.index(max(values.shape))
    beside = index_at[:main_axis] + [(index_at[main_axis] + 1) % values.shape[main_axis]] + index_at[main_axis + 1:]
    return values.at[tuple(index_at)].set(least).at[tuple(beside)].set(largest)


def block_levels(rng, extent, split, least, largest):
    factor_of = 1.0
    for dim, parts in split:
        draws = jax.random.uniform(jax.random.fold_in(jax.random.fold_in(rng, 6), dim), (parts,), jnp.float32, least / len(split), largest / len(split))
        factor_of = factor_of * jnp.repeat(jnp.exp(draws), extent[dim] // parts).reshape((-1,) + (1,) * (len(extent) - 1 - dim))
    return factor_of


def shared_out(key, own, number, rows, amount, top, bound, slope):
    order = jax.random.permutation(key, amount)
    packed, usual = portions_of(amount, rows * top, bound, slope, True), portions_of(amount, rows * top, bound, slope, False)
    places = jnp.arange(amount)

    def named(sizes, rotation):
        used = int((sizes > 0).sum())
        fixed = max(1, used // 4)
        moved = fixed + (places - fixed + rotation * (used - fixed)) % max(1, amount - fixed)
        return jnp.zeros((amount,), jnp.int32).at[order[jnp.where(places < fixed, places, moved)]].set(jnp.asarray(sizes, jnp.int32))

    sizes = jnp.where(number % 4 == 0, named(packed, number // 4), named(usual, number - number // 4 - 1))
    mixed = jax.random.permutation(jax.random.fold_in(own, 3), amount)
    source_of, taker = mixed[0:amount // 2 * 2:2], mixed[1:amount // 2 * 2:2]
    margin = jnp.minimum(sizes[source_of] - 1, bound - sizes[taker]) // 2
    margin = jnp.where((source_of == order[0]) | (taker == order[0]) | (sizes[taker] == 0), 0, jnp.maximum(margin, 0))
    moved = jax.random.randint(jax.random.fold_in(own, 4), (amount // 2,), 0, 1 << 20) % (margin + 1)
    sizes = sizes.at[source_of].add(-moved).at[taker].add(moved)
    labels = jnp.searchsorted(jnp.cumsum(sizes), jnp.arange(rows * top), side="right").astype(jnp.int32)
    table = labels.reshape(top, rows).T
    table = table[jax.random.permutation(jax.random.fold_in(own, 1), rows)]
    rotation = jax.random.randint(jax.random.fold_in(own, 2), (rows, 1), 0, top)
    return jnp.take_along_axis(table, (jnp.arange(top)[None, :] + rotation) % top, axis=1)


def portions_of(amount, total, limit, skew, full):
    loads = [(1 << 20) // math.isqrt(grade ** skew) + 1 for grade in range(1, amount + 1)]
    largest = limit if full else min(limit, max(-(-total // amount), total * loads[0] // sum(loads)))
    least = 1 if total - largest >= amount - 1 else 0
    holding, rest = [largest] + [least] * (amount - 1), total - largest - least * (amount - 1)
    while rest > 0:
        candidates = [i for i in range(1, amount) if holding[i] < largest] or [i for i in range(1, amount) if holding[i] < limit]
        whole, remaining = sum([loads[i] for i in candidates]), rest
        for i in candidates:
            addition = min(limit - holding[i], max(1, remaining * loads[i] // whole), rest)
            holding[i] = holding[i] + addition
            rest = rest - addition
    return np.array(holding)


def noise(stream_key, shape, spread, bound, split=(), kind=jnp.bfloat16):
    values = spread * jax.random.normal(stream_key, shape, jnp.float32)
    if split:
        values = values * block_levels(stream_key, shape, split, -0.22, 0.18)
    return jnp.clip(values, -bound, bound).astype(kind)


def setup_inputs(seed: int = 0) -> dict:
    splits = jax.random.split(jax.random.key(seed), 8)
    queries = draw_queries(jax.random.fold_in(splits[7], 71), 0)
    fresh_key_value = noise(splits[1], (N_GRP, GROUP_REQUESTS, DECODE_STEPS, KEY_HEADS, 2 * HEAD_WIDTH), 3.5, 16.0, ((0, 16), (3, 2)))
    key_value_cache = draw_key_value_cache(jax.random.fold_in(splits[7], 71), 0)
    lens = touch_ends(jax.random.randint(splits[3], (N_GRP, GROUP_REQUESTS), SHARD_CAPACITY, N_CTX * SHARD_CAPACITY + 1), jax.random.fold_in(splits[3], 1), SHARD_CAPACITY, N_CTX * SHARD_CAPACITY).astype(jnp.int32)
    blocks = noise(splits[4], (TOTAL_BLOCKS, BLOCK_POSITIONS, KEY_HEADS, 2 * HEAD_WIDTH), 1.0, 6.0, ((0, 256),))
    block_group_keys = jax.random.split(jax.random.fold_in(splits[5], 1), TOTAL_BLOCKS // NB)
    block_group_turns = jax.random.permutation(jax.random.fold_in(splits[5], 3), TOTAL_BLOCKS // NB)
    block_group = jax.vmap(lambda own, number: shared_out(jax.random.fold_in(splits[5], 2), own, number, NB, N_GRP, 1, MOST, 2))(block_group_keys, block_group_turns).reshape((TOTAL_BLOCKS, 1))
    block_request = touch_ends(jax.random.randint(splits[6], (TOTAL_BLOCKS,), 0, GROUP_REQUESTS), jax.random.fold_in(splits[6], 1), 0, GROUP_REQUESTS - 1).astype(jnp.int32)
    return dict(queries=queries, fresh_key_value=fresh_key_value, key_value_cache=key_value_cache, lens=lens, blocks=blocks, block_group=block_group, block_request=block_request)


def rounded(weights):
    return lax.optimization_barrier(weights.astype(jnp.bfloat16)).astype(jnp.float32)


def reference(queries, fresh_key_value, key_value_cache, lens, blocks, block_group, block_request):
    scaling = HEAD_WIDTH ** -0.5
    request_number = N_GRP * GROUP_REQUESTS
    query_entire = queries.reshape(request_number, DECODE_STEPS, KEY_HEADS, QUERY_PER_KEY, HEAD_WIDTH)
    owned_entire = fresh_key_value.reshape(request_number, DECODE_STEPS, KEY_HEADS, 2 * HEAD_WIDTH)
    cache_entire = key_value_cache.reshape(request_number, N_CTX * SHARD_CAPACITY, KEY_HEADS, 2 * HEAD_WIDTH)
    lengths = lens.reshape(request_number)
    owners = (block_group[:, 0] * GROUP_REQUESTS + block_request).astype(jnp.int32)
    causal = jnp.arange(DECODE_STEPS)[None, :] <= jnp.arange(DECODE_STEPS)[:, None]
    position = jnp.arange(N_CTX * SHARD_CAPACITY)
    block_number = N_CTX * N_GRP * N_HEAD * NB
    batch_length = math.gcd(block_number, 256)
    indices = jnp.arange(request_number)

    def request_scores(request):
        query_part = query_entire[request].astype(jnp.float32)
        cache_part = cache_entire[request].astype(jnp.float32)
        own_part = owned_entire[request].astype(jnp.float32)
        s_res = jnp.einsum('thjd,phd->thjp', query_part, cache_part[..., :HEAD_WIDTH]) * scaling
        s_own = jnp.einsum('thjd,uhd->thju', query_part, own_part[..., :HEAD_WIDTH]) * scaling
        valid = (position < lengths[request])[None, None, None, :]
        own_mask = causal[:, None, None, :]
        return s_res, s_own, valid, own_mask, cache_part, own_part

    def request_top(request):
        s_res, s_own, valid, own_mask, cache_part, own_part = request_scores(request)
        return jnp.maximum(jnp.max(jnp.where(valid, s_res, -jnp.inf), -1),
                           jnp.max(jnp.where(own_mask, s_own, -jnp.inf), -1))

    row_peak = lax.map(request_top, indices)
    grouped_rows = blocks.reshape(block_number // batch_length, batch_length, BLOCK_POSITIONS, KEY_HEADS, 2 * HEAD_WIDTH)
    owning_groups = owners.reshape(block_number // batch_length, batch_length)

    def block_scores(block_part, block_owner):
        query_part = query_entire[block_owner].astype(jnp.float32)
        key_part = block_part[..., :HEAD_WIDTH].astype(jnp.float32)
        return jnp.einsum('bthjd,bshd->bthjs', query_part, key_part) * scaling

    def block_highest(element):
        block_part, block_owner = element
        return jnp.max(block_scores(block_part, block_owner), -1)

    block_maximum = lax.map(block_highest, (grouped_rows, owning_groups)).reshape(block_number, DECODE_STEPS, KEY_HEADS, QUERY_PER_KEY)
    row_peak = jnp.maximum(row_peak, jax.ops.segment_max(block_maximum, owners, num_segments=request_number))

    def request_terms(request):
        s_res, s_own, valid, own_mask, cache_part, own_part = request_scores(request)
        peak_part = row_peak[request][..., None]
        p_res = jnp.where(valid, jnp.exp(s_res - peak_part), 0.0)
        p_own = jnp.where(own_mask, jnp.exp(s_own - peak_part), 0.0)
        weight_part = jnp.sum(p_res, -1) + jnp.sum(p_own, -1)
        combined = jnp.einsum('thjp,phd->thjd', rounded(p_res), cache_part[..., HEAD_WIDTH:])
        combined = combined + jnp.einsum('thju,uhd->thjd', rounded(p_own), own_part[..., HEAD_WIDTH:])
        return weight_part, combined

    weight_sum, accumulated = lax.map(request_terms, indices)

    def block_terms(carried, element):
        sum_part, acc_part = carried
        block_part, block_owner = element
        scores = block_scores(block_part, block_owner)
        weights = jnp.exp(scores - row_peak[block_owner][..., None])
        value_part = block_part[..., HEAD_WIDTH:].astype(jnp.float32)
        sum_part = sum_part.at[block_owner].add(jnp.sum(weights, -1))
        acc_part = acc_part.at[block_owner].add(jnp.einsum('bthjs,bshd->bthjd', rounded(weights), value_part))
        return (sum_part, acc_part), None

    (weight_sum, accumulated), unused = lax.scan(block_terms, (weight_sum, accumulated), (grouped_rows, owning_groups))
    result = (accumulated / weight_sum[..., None]).astype(jnp.bfloat16)
    return result.reshape(queries.shape)
```

```python
import functools

import jax
import jax.numpy as jnp
from jax import lax
from jax.experimental import pallas as pl
from jax.experimental.pallas import tpu as pltpu
from jax.sharding import PartitionSpec as P

NONE = -1e30
X, Y, Z = 4, 4, 8
LOG2E = 1.4426950408889634
VMEM = pl.BlockSpec(memory_space=pltpu.VMEM)
SMEM = pl.BlockSpec(memory_space=pltpu.SMEM)
bf16, f32 = jnp.bfloat16, jnp.float32


def place(x, y, z):
    return ((y % 2) * X + x) * (2 * Z) + (y // 2) * Z + z


def swapped(value, dx=0, dy=0, dz=0):
    route = [
        (place(x, y, z), place(x ^ dx, y ^ dy, z ^ dz))
        for x in range(X)
        for y in range(Y)
        for z in range(Z)
    ]
    return lax.ppermute(value, ("ctx", "grp"), route)


def iota(shape, dim):
    return lax.broadcasted_iota(jnp.int32, shape, dim)


def split3(value):
    high = value.astype(bf16)
    rest = value - high.astype(f32)
    middle = rest.astype(bf16)
    low = (rest - middle.astype(f32)).astype(bf16)
    return high, middle, low


def scores(q, k):
    return lax.dot_general(q, k, (((1,), (1,)), ((), ())), preferred_element_type=f32)


def fresh_kernel(q_ref, kv_ref, o_ref, lse_ref):
    s = scores(q_ref[...], kv_ref[:, :128]) * (128**-0.5 * LOG2E)
    row, col = iota(s.shape, 0), iota(s.shape, 1)
    valid = (row // 32 == col // 16) & (row % 4 == col % 4) & ((col % 16) // 4 <= (row % 16) // 4)
    s = jnp.where(valid, s, NONE)
    m = jnp.max(s, axis=1, keepdims=True)
    p = jnp.exp2(s - m)
    l = jnp.sum(p, axis=1, keepdims=True)
    acc = jnp.dot(p.astype(bf16), kv_ref[:, 128:], preferred_element_type=f32)
    o_ref[...] = (acc / l).astype(bf16)
    lse = jnp.broadcast_to(m + jnp.log2(l), (128, 128))
    eye = iota((128, 128), 0) == iota((128, 128), 1)
    lse_ref[...] = jnp.broadcast_to(jnp.sum(jnp.where(eye, lse, 0.0), axis=0, keepdims=True), (8, 128))


def main_kernel(scal, keys, *refs):
    qa, qb = refs[0:4], refs[4:8]
    blk, cache = refs[8], refs[9]
    pa, pb = refs[10:14], refs[14:18]
    ids, cnt, bias, m_s, l_s, acc_s, lse_a, lse_b = refs[18:]
    scale = 128**-0.5 * LOG2E
    group, ctx = scal[0], scal[1]

    def clear(i, _):
        cnt[i] = 0
        for j in range(16):
            ids[i * 16 + j] = 0
        return 0

    lax.fori_loop(0, 64, clear, 0)

    def enter(i, _):
        k = keys[i]
        c = cnt[k]
        ids[k * 16 + jnp.minimum(c, 15)] = i
        cnt[k] = c + 1
        return 0

    lax.fori_loop(0, 128, enter, 0)

    row, lane = iota((256, 256), 0), iota((256, 256), 1)
    same_head = row % 4 == lane % 4
    for n in range(5):
        bias[n] = jnp.where(same_head & (lane < n * 64), 0.0, NONE)
    lse_a[...] = jnp.zeros_like(lse_a)
    lse_b[...] = jnp.zeros_like(lse_b)
    ones = jnp.ones((256, 128), bf16)

    def queries_of(dyhi, dz, r):
        tiles = []
        for dylo in range(2):
            for dx in range(X):
                if r < 2:
                    ref, slot = qa[2 * dyhi + dylo], dx * Z + dz
                else:
                    ref, slot = qb[dx], (2 * dyhi + dylo) * Z + dz
                tiles.append(ref[pl.ds(pl.multiple_of(slot * 64 + (r % 2) * 32, 32), 32), :])
        return jnp.concatenate(tiles, axis=0)

    def weighted(s, m, v):
        p = jnp.exp2(s - m).astype(bf16)
        both = jnp.dot(p, jnp.concatenate([ones, v], axis=1), preferred_element_type=f32)
        return both[:, :128], both[:, 128:]

    def update(r, s, v):
        m_old = m_s[r]
        m_new = jnp.maximum(m_old, jnp.max(s, axis=1, keepdims=True))
        l, acc = weighted(s, m_new[:, :1], v)
        a = jnp.exp2(m_old - m_new)
        m_s[r] = m_new
        l_s[r] = l_s[r] * a + l
        acc_s[r] = acc_s[r] * a + acc

    def tiles_of(k, start):
        return jnp.concatenate([blk[ids[k * 16 + start + j]] for j in range(4)], axis=0)

    def body(dyhi, dz, own):
        their = lax.bitwise_xor(group, dyhi * Z + dz)
        queries = [queries_of(dyhi, dz, r) for r in range(4)]
        for r in range(4):
            k = their * 4 + r
            kv = tiles_of(k, 0)
            s = scores(queries[r], kv[:, :128]) * scale + bias[jnp.minimum(cnt[k], 4)]
            m = jnp.max(s, axis=1, keepdims=True)
            l, acc = weighted(s, m, kv[:, 128:])
            m_s[r] = jnp.broadcast_to(m, (256, 128))
            l_s[r] = l
            acc_s[r] = acc
        for r in range(4):
            k = their * 4 + r
            count = cnt[k]

            @pl.when(count > 4)
            def _():
                def more(c, _):
                    kv = tiles_of(k, c * 4)
                    s = scores(queries[r], kv[:, :128]) * scale + bias[jnp.minimum(count - c * 4, 4)]
                    update(r, s, kv[:, 128:])
                    return 0

                lax.fori_loop(1, (count + 3) // 4, more, 0)

        if own:
            here = [jnp.clip(scal[2 + r] - ctx * 512, 0, 512) for r in range(4)]
            longest = jnp.maximum(jnp.maximum(here[0], here[1]), jnp.maximum(here[2], here[3]))

            def resident(c, _):
                for r in range(4):
                    kv = cache[r, pl.ds(pl.multiple_of(c * 256, 256), 256), :]
                    s = scores(queries[r], kv[:, :128]) * scale + bias[4]
                    s = jnp.where(lane < (here[r] - c * 64) * 4, s, NONE)
                    update(r, s, kv[:, 128:])
                return 0

            lax.fori_loop(0, (longest + 63) // 64, resident, 0)
        r_of, l_of = iota((256, 128), 0) % 32, iota((256, 128), 1)
        for r in range(4):
            l = l_s[r]
            o = (acc_s[r] / l).astype(bf16)
            lse = m_s[r] + jnp.log2(l)
            at = r_of + ((dz % 2) * 64 + (r % 2) * 32)
            lse = jnp.sum(jnp.where(l_of == at, lse, 0.0).reshape(8, 32, 128), axis=1)
            for i in range(8):
                dy, dx = 2 * dyhi + i // 4, i % 4
                tile = o[i * 32 : (i + 1) * 32]
                if r < 2:
                    out, slot, kept, at_kept = pa[dx], dy * Z + dz, lse_a.at[dx], dy * 4 + dz // 2
                else:
                    out, slot, kept, at_kept = pb[dy], dx * Z + dz, lse_b.at[dy], dx * 4 + dz // 2
                out[pl.ds(pl.multiple_of(slot * 64 + (r % 2) * 32, 32), 32), :] = tile
                kept[pl.ds(at_kept, 1), :] += lse[i : i + 1]

    body(0, 0, True)

    def low(dz, _):
        body(0, dz, False)
        return 0

    def high(dz, _):
        body(1, dz, False)
        return 0

    lax.fori_loop(1, Z, low, 0)
    lax.fori_loop(0, Z, high, 0)
    for outs, kept in ((pa, lse_a), (pb, lse_b)):
        for i in range(4):
            for j, part in enumerate(split3(kept[i])):
                outs[i][2048 + 16 * j : 2064 + 16 * j, :] = part


def shares(lses):
    top = functools.reduce(jnp.maximum, lses)
    parts = [jnp.exp2(l - top) for l in lses]
    total = functools.reduce(jnp.add, parts)
    return [p / total for p in parts], top + jnp.log2(total)


def mixed(weights, tiles, eye):
    scales = jnp.concatenate([jnp.where(eye, w, 0.0).astype(bf16) for w in weights], axis=1)
    return jnp.dot(scales, jnp.concatenate(tiles, axis=0), preferred_element_type=f32)


def lse_at(ref, start, rows):
    tail = ref[start:, :].astype(f32)
    return tail[0:rows] + tail[rows : 2 * rows] + tail[2 * rows : 3 * rows]


def packed(parts):
    rows = sum(p.shape[0] for p in parts)
    return jnp.concatenate(parts + [jnp.zeros((16 - rows, 128), f32)], axis=0).astype(bf16)


def parts_f32(lse):
    return [p.astype(f32) for p in split3(lse)]


def first_kernel(*refs):
    eye = iota((128, 128), 0) == iota((128, 128), 1)
    for half in range(2):
        ins, outs = refs[4 * half : 4 * half + 4], refs[8 + 4 * half : 12 + 4 * half]
        weights, lse = shares([lse_at(ref, 2048, 16) for ref in ins])
        for p in range(16):
            rows = slice(p * 128, (p + 1) * 128)
            o = mixed([w[p : p + 1] for w in weights], [ref[rows, :] for ref in ins], eye)
            outs[p // 4][(p % 4) * 128 : (p % 4 + 1) * 128, :] = o.astype(bf16)
        for i in range(4):
            outs[i][512:528, :] = packed(parts_f32(lse[4 * i : 4 * i + 4]))


def second_kernel(*refs):
    eye = iota((128, 128), 0) == iota((128, 128), 1)
    outs = refs[8:16]
    halves = []
    for half in range(2):
        ins = refs[4 * half : 4 * half + 4]
        weights, lse = shares([lse_at(ref, 512, 4) for ref in ins])
        for p in range(4):
            rows = slice(p * 128, (p + 1) * 128)
            o = mixed([w[p : p + 1] for w in weights], [ref[rows, :] for ref in ins], eye).astype(bf16)
            for i in range(2):
                outs[2 * p + i][64 * half : 64 * half + 64, :] = o[64 * i : 64 * i + 64]
        halves.append(parts_f32(lse))
    for dz in range(Z):
        p = dz // 2
        outs[dz][128:144, :] = packed([part[p : p + 1] for half in halves for part in half])


def last_kernel(*refs):
    eye = iota((128, 128), 0) == iota((128, 128), 1)
    left = iota((1, 128), 1) < 64
    ins, o_fresh, lse_fresh, out = refs[:Z], refs[Z], refs[Z + 1], refs[Z + 2]
    lses = []
    for dz in range(Z):
        tail = ins[dz][128:144, :].astype(f32)
        a = tail[0:1] + tail[1:2] + tail[2:3]
        b = tail[3:4] + tail[4:5] + tail[5:6]
        moved = pltpu.roll(jnp.broadcast_to(a if dz % 2 else b, (8, 128)), 64, 1)[0:1]
        lses.append(jnp.where(left, moved, b) if dz % 2 else jnp.where(left, a, moved))
    weights, _ = shares(lses + [lse_fresh[0:1, :]])
    tiles = [ref[0:128, :] for ref in ins] + [o_fresh[...]]
    out[...] = mixed(weights, tiles, eye).astype(bf16)


def call(kernel, outs, ins, scratch=(), specs=None, flops=0, size=0):
    shapes = [jax.ShapeDtypeStruct(s, d) for s, d in outs]
    return pl.pallas_call(
        kernel,
        out_shape=shapes,
        in_specs=specs or [VMEM] * len(ins),
        out_specs=[VMEM] * len(outs),
        scratch_shapes=list(scratch),
        compiler_params=pltpu.CompilerParams(vmem_limit_bytes=48 << 20),
        cost_estimate=pl.CostEstimate(flops=flops, bytes_accessed=size, transcendentals=0),
    )(*ins)


def body(queries, fresh_key_value, key_value_cache, lens, blocks, block_group, block_request):
    ctx, grp, head = (lax.axis_index(a) for a in ("ctx", "grp", "head"))
    q = queries.reshape(4, 16, 2, 128).transpose(0, 2, 1, 3).reshape(2, 1, 64, 128)

    near = jnp.concatenate([q, swapped(q, dz=1)], axis=1)
    line = jnp.concatenate([near] + [swapped(near, dz=d) for d in (2, 4, 6)], axis=1)
    line_a, line_b = line[0].reshape(512, 128), line[1].reshape(512, 128)
    plane_a = jnp.concatenate([line_a] + [swapped(line_a, dx=d) for d in (1, 2, 3)], axis=0)
    plane_b = jnp.concatenate([line_b] + [swapped(line_b, dy=d) for d in (1, 2, 3)], axis=0)
    qa = [plane_a] + [swapped(plane_a, dy=d) for d in (1, 2, 3)]
    qb = [plane_b] + [swapped(plane_b, dx=d) for d in (1, 2, 3)]

    halves = blocks.reshape(64, 16, 2, 4, 256)
    mine = lax.dynamic_index_in_dim(halves, head, 2, keepdims=False).reshape(64, 64, 256)
    other = lax.dynamic_index_in_dim(halves, 1 - head, 2, keepdims=False).reshape(64, 64, 256)
    key = block_group[:, 0] * 4 + block_request
    pair = [(0, 1), (1, 0)]
    blk = jnp.concatenate([mine, lax.ppermute(other, "head", pair)], axis=0)
    keys = jnp.concatenate([key, lax.ppermute(key, "head", pair)], axis=0)
    cache = key_value_cache.reshape(4, 2048, 256)
    scal = jnp.concatenate([jnp.stack([grp, ctx]).astype(jnp.int32), lens[0]])

    o_fresh, lse_fresh = call(
        fresh_kernel, [((128, 128), bf16), ((8, 128), f32)], [q.reshape(128, 128), fresh_key_value.reshape(64, 256)]
    )
    partial = call(
        main_kernel,
        [((2096, 128), bf16)] * 8,
        [scal, keys, *qa, *qb, blk, cache],
        scratch=[
            pltpu.SMEM((1024,), jnp.int32),
            pltpu.SMEM((64,), jnp.int32),
            pltpu.VMEM((5, 256, 256), f32),
            pltpu.VMEM((4, 256, 128), f32),
            pltpu.VMEM((4, 256, 128), f32),
            pltpu.VMEM((4, 256, 128), f32),
            pltpu.VMEM((4, 16, 128), f32),
            pltpu.VMEM((4, 16, 128), f32),
        ],
        specs=[SMEM, SMEM] + [VMEM] * 10,
        flops=4 << 30,
        size=16 << 20,
    )
    pa, pb = partial[:4], partial[4:]
    pa = [pa[0]] + [swapped(pa[d], dx=d) for d in (1, 2, 3)]
    pb = [pb[0]] + [swapped(pb[d], dy=d) for d in (1, 2, 3)]
    lines = call(first_kernel, [((528, 128), bf16)] * 8, [*pa, *pb], flops=1 << 28, size=6 << 20)
    ca, cb = lines[:4], lines[4:]
    ca = [ca[0]] + [swapped(ca[d], dy=d) for d in (1, 2, 3)]
    cb = [cb[0]] + [swapped(cb[d], dx=d) for d in (1, 2, 3)]
    points = call(second_kernel, [((144, 128), bf16)] * 8, [*ca, *cb], flops=1 << 26, size=2 << 20)
    points = [points[0]] + [swapped(points[d], dz=d) for d in range(1, 8)]
    (out,) = call(last_kernel, [((128, 128), bf16)], [*points, o_fresh, lse_fresh], flops=1 << 25, size=1 << 19)
    return out.reshape(4, 2, 16, 128).transpose(0, 2, 1, 3).reshape(queries.shape)


def solution(mesh):
    return jax.shard_map(
        body,
        mesh=mesh,
        in_specs=(
            P("grp", None, None, "head", "ctx"),
            P("grp", None, None, "head", None),
            P("grp", None, "ctx", "head", None),
            P("grp", None),
            P(("ctx", "grp", "head"), None, None, None),
            P(("ctx", "grp", "head"), None),
            P(("ctx", "grp", "head")),
        ),
        out_specs=P("grp", None, None, "head", "ctx"),
        check_vma=False,
    )
```

```python
import functools

import jax
import jax.numpy as jnp
from jax import lax
from jax.experimental import pallas as pl
from jax.experimental.pallas import tpu as pltpu
from jax.sharding import PartitionSpec as P

NONE = -1e30
X, Y, Z = 4, 4, 8
LOG2E = 1.4426950408889634
VMEM = pl.BlockSpec(memory_space=pltpu.VMEM)
SMEM = pl.BlockSpec(memory_space=pltpu.SMEM)
bf16, f32 = jnp.bfloat16, jnp.float32


def place(x, y, z):
    return ((y % 2) * X + x) * (2 * Z) + (y // 2) * Z + z


def swapped(value, dx=0, dy=0, dz=0):
    route = [
        (place(x, y, z), place(x ^ dx, y ^ dy, z ^ dz))
        for x in range(X)
        for y in range(Y)
        for z in range(Z)
    ]
    return lax.ppermute(value, ("ctx", "grp"), route)


def iota(shape, dim):
    return lax.broadcasted_iota(jnp.int32, shape, dim)


def split3(value):
    high = value.astype(bf16)
    rest = value - high.astype(f32)
    middle = rest.astype(bf16)
    low = (rest - middle.astype(f32)).astype(bf16)
    return high, middle, low


def scores(q, k):
    return lax.dot_general(q, k, (((1,), (1,)), ((), ())), preferred_element_type=f32)


def fresh_kernel(q_ref, kv_ref, o_ref, lse_ref):
    s = scores(q_ref[...], kv_ref[:, :128]) * (128**-0.5 * LOG2E)
    row, col = iota(s.shape, 0), iota(s.shape, 1)
    valid = (row // 32 == col // 16) & (row % 4 == col % 4) & ((col % 16) // 4 <= (row % 16) // 4)
    s = jnp.where(valid, s, NONE)
    m = jnp.max(s, axis=1, keepdims=True)
    p = jnp.exp2(s - m)
    l = jnp.sum(p, axis=1, keepdims=True)
    acc = jnp.dot(p.astype(bf16), kv_ref[:, 128:], preferred_element_type=f32)
    o_ref[...] = (acc / l).astype(bf16)
    lse = jnp.broadcast_to(m + jnp.log2(l), (128, 128))
    eye = iota((128, 128), 0) == iota((128, 128), 1)
    lse_ref[...] = jnp.broadcast_to(jnp.sum(jnp.where(eye, lse, 0.0), axis=0, keepdims=True), (8, 128))


def index_kernel(keys, ids, cnt):
    def clear(i, _):
        cnt[i] = 0
        for j in range(16):
            ids[i * 16 + j] = 0
        return 0

    lax.fori_loop(0, 64, clear, 0)

    def enter(i, _):
        k = keys[i]
        c = cnt[k]
        ids[k * 16 + jnp.minimum(c, 15)] = i
        cnt[k] = c + 1
        return 0

    lax.fori_loop(0, 128, enter, 0)


def piece_kernel(d, scal, ids, cnt, qa, qb, blk, cache, pa, pb, bias, ma, la, acca, mb, lb, accb, lse_a, lse_b):
    scale = 128**-0.5 * LOG2E
    group, ctx = scal[0], scal[1]
    row, lane = iota((8, 256), 0), iota((8, 256), 1)
    for n in range(5):
        bias[n] = jnp.where((row % 4 == lane % 4) & (lane < n * 64), 0.0, NONE)
    ones = jnp.ones((256, 128), bf16)
    units = []
    for r in range(2):
        units.append((qa, [dx * Z for dx in range(X)], r, d // 2, ma.at[r], la.at[r], acca.at[r], pa, lse_a))
    for r in range(2, 4):
        for dyhi in range(2):
            i = 2 * (r - 2) + dyhi
            slots = [(2 * dyhi + dylo) * Z for dylo in range(2)]
            units.append((qb, slots, r, dyhi, mb.at[i], lb.at[i], accb.at[i], pb, lse_b))

    def rows_at(slot, dz, r):
        return pl.ds(pl.multiple_of((slot + dz) * 64 + (r % 2) * 32, 32), 32)

    def scaled(q, k, extra):
        s = scores(q, k)
        return (s.reshape(-1, 8, 256) * scale + extra[None]).reshape(s.shape)

    def weighted(s, m, v):
        p = jnp.exp2(s - m).astype(bf16)
        both = jnp.dot(p, jnp.concatenate([ones, v], axis=1), preferred_element_type=f32)
        return both[:, :128], both[:, 128:]

    def update(m_ref, l_ref, acc_ref, s, v):
        m_old = m_ref[...]
        m_new = jnp.maximum(m_old, jnp.max(s, axis=1, keepdims=True))
        l, acc = weighted(s, m_new[:, :1], v)
        a = jnp.exp2(m_old - m_new)
        m_ref[...] = m_new
        l_ref[...] = l_ref[...] * a + l
        acc_ref[...] = acc_ref[...] * a + acc

    def tiles_of(k, start):
        return jnp.concatenate([blk[ids[k * 16 + start + j]] for j in range(4)], axis=0)

    def body(dz, own):
        queries, keys = [], []
        for ref, slots, r, dyhi, m_ref, l_ref, acc_ref, _, _ in units:
            q = jnp.concatenate([ref[rows_at(s, dz, r), :] for s in slots], axis=0)
            k = lax.bitwise_xor(group, dyhi * Z + dz) * 4 + r
            kv = tiles_of(k, 0)
            s = scaled(q, kv[:, :128], bias[jnp.minimum(cnt[k], 4)])
            m = jnp.max(s, axis=1, keepdims=True)
            l, acc = weighted(s, m, kv[:, 128:])
            m_ref[...] = jnp.broadcast_to(m, m_ref.shape)
            l_ref[...] = l
            acc_ref[...] = acc
            queries.append(q)
            keys.append(k)
        for q, k, (_, _, _, _, m_ref, l_ref, acc_ref, _, _) in zip(queries, keys, units):
            count = cnt[k]

            @pl.when(count > 4)
            def _():
                def more(c, _):
                    kv = tiles_of(k, c * 4)
                    s = scaled(q, kv[:, :128], bias[jnp.minimum(count - c * 4, 4)])
                    update(m_ref, l_ref, acc_ref, s, kv[:, 128:])
                    return 0

                lax.fori_loop(1, (count + 3) // 4, more, 0)

        if own:
            mine = [(q, u) for q, u in zip(queries, units) if u[3] == 0]
            here = {u[2]: jnp.clip(scal[2 + u[2]] - ctx * 512, 0, 512) for _, u in mine}
            longest = functools.reduce(jnp.maximum, here.values())

            def resident(c, _):
                for q, u in mine:
                    r = u[2]
                    kv = cache[r, pl.ds(pl.multiple_of(c * 256, 256), 256), :]
                    limit = jnp.where(lane < (here[r] - c * 64) * 4, bias[4], NONE)
                    update(u[4], u[5], u[6], scaled(q, kv[:, :128], limit), kv[:, 128:])
                return 0

            lax.fori_loop(0, (longest + 63) // 64, resident, 0)
        for _, slots, r, _, m_ref, l_ref, acc_ref, out, kept in units:
            l = l_ref[...]
            o = (acc_ref[...] / l).astype(bf16)
            lse = m_ref[...] + jnp.log2(l)
            at = iota(l.shape, 0) % 32 + ((dz % 2) * 64 + (r % 2) * 32)
            lse = jnp.where(iota(l.shape, 1) == at, lse, 0.0)
            lse = jnp.sum(lse.reshape(len(slots), 32, 128), axis=1)
            for i, slot in enumerate(slots):
                out[rows_at(slot, dz, r), :] = o[i * 32 : (i + 1) * 32]
                kept[pl.ds(slot // 2 + dz // 2, 1), :] += lse[i : i + 1]

    lse_a[...] = jnp.zeros_like(lse_a)
    lse_b[...] = jnp.zeros_like(lse_b)
    body(0, True)

    def rest(dz, _):
        body(dz, False)
        return 0

    lax.fori_loop(1, Z, rest, 0)
    for out, kept in ((pa, lse_a), (pb, lse_b)):
        for j, part in enumerate(split3(kept[...])):
            out[2048 + 16 * j : 2064 + 16 * j, :] = part


def shares(lses):
    top = functools.reduce(jnp.maximum, lses)
    parts = [jnp.exp2(l - top) for l in lses]
    total = functools.reduce(jnp.add, parts)
    return [p / total for p in parts], top + jnp.log2(total)


def mixed(weights, tiles):
    eye = iota((128, 128), 0) == iota((128, 128), 1)
    scales = jnp.concatenate([jnp.where(eye, w, 0.0).astype(bf16) for w in weights], axis=1)
    return jnp.dot(scales, jnp.concatenate(tiles, axis=0), preferred_element_type=f32)


def lse_of(ref, n):
    tail = ref[128 * n :, :].astype(f32)
    return tail[0:n] + tail[n : 2 * n] + tail[2 * n : 3 * n]


def put_lse(ref, lse):
    n = lse.shape[0]
    rows = [p.astype(f32) for p in split3(lse)]
    rows.append(jnp.zeros((16 - 3 * n, 128), f32))
    ref[128 * n :, :] = jnp.concatenate(rows, axis=0).astype(bf16)


def merged(ins, n):
    weights, lse = shares([lse_of(ref, n) for ref in ins])
    outs = []
    for p in range(n):
        o = mixed([w[p : p + 1] for w in weights], [ref[p * 128 : (p + 1) * 128, :] for ref in ins])
        outs.append(o.astype(bf16))
    return outs, lse


def put(outs, tiles, lse):
    n = len(tiles) // len(outs)
    for i, out in enumerate(outs):
        for j in range(n):
            out[j * 128 : (j + 1) * 128, :] = tiles[i * n + j]
        put_lse(out, lse[i * n : (i + 1) * n])


def plane_kernel(*refs):
    for half in range(2):
        put(refs[8 + 4 * half : 12 + 4 * half], *merged(refs[4 * half : 4 * half + 4], 16))


def line_kernel(*refs):
    left = iota((4, 128), 1) < 64
    (a, lse_a), (b, lse_b) = merged(refs[:4], 4), merged(refs[4:8], 4)

    def turned(lse):
        return pltpu.roll(jnp.concatenate([lse, lse], axis=0), 64, 1)[0:4]

    even = jnp.where(left, lse_a, turned(lse_b))
    odd = jnp.where(left, turned(lse_a), lse_b)
    tiles, rows = [], []
    for p in range(4):
        for i, lse in ((0, even), (1, odd)):
            half = slice(64 * i, 64 * i + 64)
            tiles.append(jnp.concatenate([a[p][half], b[p][half]], axis=0))
            rows.append(lse[p : p + 1])
    put(refs[8:10], tiles, jnp.concatenate(rows, axis=0))


def halve_kernel(n, one, two, low, high):
    put((low, high), *merged((one, two), n))


def last_kernel(one, two, o_fresh, lse_fresh, out):
    weights, _ = shares([lse_of(one, 1), lse_of(two, 1), lse_fresh[0:1, :]])
    out[...] = mixed(weights, [one[0:128, :], two[0:128, :], o_fresh[...]]).astype(bf16)


def call(kernel, outs, ins, scratch=(), specs=None, out_specs=None, flops=0, size=0):
    shapes = [jax.ShapeDtypeStruct(s, d) for s, d in outs]
    return pl.pallas_call(
        kernel,
        out_shape=shapes,
        in_specs=specs or [VMEM] * len(ins),
        out_specs=out_specs or [VMEM] * len(outs),
        scratch_shapes=list(scratch),
        compiler_params=pltpu.CompilerParams(vmem_limit_bytes=40 << 20),
        cost_estimate=pl.CostEstimate(flops=flops, bytes_accessed=size, transcendentals=0),
    )(*ins)


def body(queries, fresh_key_value, key_value_cache, lens, blocks, block_group, block_request):
    ctx, grp, head = (lax.axis_index(a) for a in ("ctx", "grp", "head"))
    q = queries.reshape(4, 16, 2, 128).transpose(0, 2, 1, 3).reshape(2, 1, 64, 128)

    line = jnp.concatenate([q, swapped(q, dz=1)], axis=1)
    line, blocks, block_group, block_request, key_value_cache, fresh_key_value = lax.optimization_barrier(
        (line, blocks, block_group, block_request, key_value_cache, fresh_key_value)
    )
    line = jnp.concatenate([line, swapped(line, dz=2)], axis=1)
    line = jnp.concatenate([line, swapped(line, dz=4)], axis=1)
    line_a, line_b = line[0].reshape(512, 128), line[1].reshape(512, 128)
    plane_a = jnp.concatenate([line_a] + [swapped(line_a, dx=d) for d in (1, 2, 3)], axis=0)
    plane_b = jnp.concatenate([line_b] + [swapped(line_b, dy=d) for d in (1, 2, 3)], axis=0)
    qa, qb = {0: plane_a}, {0: plane_b}
    for d in (1, 3, 2):
        qa[d] = swapped(plane_a, dy=d)
        qb[d] = swapped(plane_b, dx=d)

    mine = lax.dynamic_slice_in_dim(blocks, 4 * head, 4, 2).reshape(64, 64, 256)
    other = lax.dynamic_slice_in_dim(blocks, 4 - 4 * head, 4, 2).reshape(64, 64, 256)
    key = block_group[:, 0] * 4 + block_request
    pair = [(0, 1), (1, 0)]
    blk = jnp.concatenate([mine, lax.ppermute(other, "head", pair)], axis=0)
    keys = jnp.concatenate([key, lax.ppermute(key, "head", pair)], axis=0)
    cache = key_value_cache.reshape(4, 2048, 256)
    scal = jnp.concatenate([jnp.stack([grp, ctx]).astype(jnp.int32), lens[0]])
    ids, cnt = call(
        index_kernel, [((1024,), jnp.int32), ((64,), jnp.int32)], [keys], specs=[SMEM], out_specs=[SMEM] * 2
    )
    o_fresh, lse_fresh = call(
        fresh_kernel, [((128, 128), bf16), ((8, 128), f32)], [q.reshape(128, 128), fresh_key_value.reshape(64, 256)]
    )
    pa, pb = {}, {}
    for d in (0, 1, 3, 2):
        pa[d], pb[d] = call(
            functools.partial(piece_kernel, d),
            [((2096, 128), bf16)] * 2,
            [scal, ids, cnt, qa[d], qb[d], blk, cache],
            scratch=[pltpu.VMEM((5, 8, 256), f32)]
            + [pltpu.VMEM((2, 128, 128), f32)] * 3
            + [pltpu.VMEM((4, 64, 128), f32)] * 3
            + [pltpu.VMEM((16, 128), f32)] * 2,
            specs=[SMEM] * 3 + [VMEM] * 4,
            flops=8 << 30,
            size=10 << 20,
        )
        pa[d], pb[d] = (swapped(pa[d], dy=d), swapped(pb[d], dx=d)) if d else (pa[d], pb[d])
    lines = call(
        plane_kernel, [((528, 128), bf16)] * 8, [pa[d] for d in range(4)] + [pb[d] for d in range(4)], size=6 << 20
    )
    ca = [lines[0]] + [swapped(lines[d], dx=d) for d in (1, 2, 3)]
    cb = [lines[4]] + [swapped(lines[4 + d], dy=d) for d in (1, 2, 3)]
    low, high = call(line_kernel, [((528, 128), bf16)] * 2, [*ca, *cb], size=2 << 20)
    low, high = call(functools.partial(halve_kernel, 4), [((272, 128), bf16)] * 2, [low, swapped(high, dz=4)])
    low, high = call(functools.partial(halve_kernel, 2), [((144, 128), bf16)] * 2, [low, swapped(high, dz=2)])
    (out,) = call(last_kernel, [((128, 128), bf16)], [low, swapped(high, dz=1), o_fresh, lse_fresh])
    return out.reshape(4, 2, 16, 128).transpose(0, 2, 1, 3).reshape(queries.shape)


def solution(mesh):
    return jax.shard_map(
        body,
        mesh=mesh,
        in_specs=(
            P("grp", None, None, "head", "ctx"),
            P("grp", None, None, "head", None),
            P("grp", None, "ctx", "head", None),
            P("grp", None),
            P(("ctx", "grp", "head"), None, None, None),
            P(("ctx", "grp", "head"), None),
            P(("ctx", "grp", "head")),
        ),
        out_specs=P("grp", None, None, "head", "ctx"),
        check_vma=False,
    )
```

```python
import functools

import jax
import jax.numpy as jnp
from jax import lax
from jax.experimental import pallas as pl
from jax.experimental.pallas import tpu as pltpu
from jax.sharding import PartitionSpec as P

NONE = -1e30
X, Y, Z = 4, 4, 8
LOG2E = 1.4426950408889634
VMEM = pl.BlockSpec(memory_space=pltpu.VMEM)
SMEM = pl.BlockSpec(memory_space=pltpu.SMEM)
bf16, f32 = jnp.bfloat16, jnp.float32


def place(x, y, z):
    return ((y % 2) * X + x) * (2 * Z) + (y // 2) * Z + z


def swapped(value, dx=0, dy=0, dz=0):
    route = [
        (place(x, y, z), place(x ^ dx, y ^ dy, z ^ dz))
        for x in range(X)
        for y in range(Y)
        for z in range(Z)
    ]
    return lax.ppermute(value, ("ctx", "grp"), route)


def iota(shape, dim):
    return lax.broadcasted_iota(jnp.int32, shape, dim)


def split3(value):
    high = value.astype(bf16)
    rest = value - high.astype(f32)
    middle = rest.astype(bf16)
    low = (rest - middle.astype(f32)).astype(bf16)
    return high, middle, low


def scores(q, k):
    return lax.dot_general(q, k, (((1,), (1,)), ((), ())), preferred_element_type=f32)


def fresh_kernel(q_ref, kv_ref, o_ref, lse_ref):
    s = scores(q_ref[...], kv_ref[:, :128]) * (128**-0.5 * LOG2E)
    row, col = iota(s.shape, 0), iota(s.shape, 1)
    valid = (row // 32 == col // 16) & (row % 4 == col % 4) & ((col % 16) // 4 <= (row % 16) // 4)
    s = jnp.where(valid, s, NONE)
    m = jnp.max(s, axis=1, keepdims=True)
    p = jnp.exp2(s - m)
    l = jnp.sum(p, axis=1, keepdims=True)
    acc = jnp.dot(p.astype(bf16), kv_ref[:, 128:], preferred_element_type=f32)
    o_ref[...] = (acc / l).astype(bf16)
    lse = jnp.broadcast_to(m + jnp.log2(l), (128, 128))
    eye = iota((128, 128), 0) == iota((128, 128), 1)
    lse_ref[...] = jnp.broadcast_to(jnp.sum(jnp.where(eye, lse, 0.0), axis=0, keepdims=True), (8, 128))


def index_kernel(keys, ids, cnt, over, nover):
    def clear(i, _):
        cnt[i] = 0
        for j in range(16):
            ids[i * 16 + j] = 0
        over[2 * i] = 0
        over[2 * i + 1] = 0
        return 0

    lax.fori_loop(0, 64, clear, 0)
    for i in range(4):
        nover[i] = 0

    def enter(i, _):
        k = keys[i]
        c = cnt[k]
        ids[k * 16 + jnp.minimum(c, 15)] = i
        cnt[k] = c + 1
        return 0

    lax.fori_loop(0, 128, enter, 0)

    def beyond(k, _):
        which = (k // 32) * 2 + (k % 4) // 2

        def more(c, _):
            n = nover[which]
            over[which * 32 + jnp.minimum(n, 31)] = k * 4 + c
            nover[which] = n + 1
            return 0

        lax.fori_loop(1, (jnp.minimum(cnt[k], 16) + 3) // 4, more, 0)
        return 0

    lax.fori_loop(0, 64, beyond, 0)


def piece_kernel(half, d, scal, ids, cnt, over, nover, *refs):
    n = 1 + half
    q_refs, (blk, cache), outs = refs[:n], refs[n : n + 2], refs[n + 2 : 2 * n + 2]
    bias, st_m, st_l, st_acc, kept = refs[2 * n + 2 :]
    scale = 128**-0.5 * LOG2E
    group, ctx = scal[0], scal[1]
    row, lane = iota((8, 256), 0), iota((8, 256), 1)
    for i in range(5):
        bias[i] = jnp.where((row % 4 == lane % 4) & (lane < i * 64), 0.0, NONE)
    ones = jnp.ones((256, 128), bf16)
    unit_count = 16 * n
    spare = unit_count

    def places(dyhi, dz, r2):
        if half:
            slots = [(i, (2 * dyhi + dylo) * Z + dz) for i in range(2) for dylo in range(2)]
        else:
            slots = [(0, dx * Z + dz) for dx in range(X)]
        return [(i, pl.ds(pl.multiple_of(s * 64 + r2 * 32, 32), 32)) for i, s in slots]

    def queries_of(dyhi, dz, r2):
        return jnp.concatenate([q_refs[i][rows, :] for i, rows in places(dyhi, dz, r2)], axis=0)

    def unit_of(dyhi, dz, r2):
        return (dyhi * Z + dz) * 2 + r2 if half else dz * 2 + r2

    def tiles_of(k, start):
        return jnp.concatenate([blk[ids[k * 16 + start + j]] for j in range(4)], axis=0)

    def store_partial(u, q, kv, extra):
        s = scores(q, kv[:, :128])
        s = (s.reshape(16, 8, 256) * scale + extra[None]).reshape(128, 256)
        m = jnp.max(s, axis=1, keepdims=True)
        p = jnp.exp2(s - m).astype(bf16)
        both = jnp.dot(p, jnp.concatenate([ones, kv[:, 128:]], axis=1), preferred_element_type=f32)
        st_m[u] = jnp.broadcast_to(m, (128, 128))
        st_l[u] = both[:, :128]
        st_acc[u] = both[:, 128:]

    def merge(u, others):
        ms = [st_m[i] for i in [u, *others]]
        top = functools.reduce(jnp.maximum, ms)
        ws = [jnp.exp2(m - top) for m in ms]
        l = functools.reduce(jnp.add, [w * st_l[i] for w, i in zip(ws, [u, *others])])
        acc = functools.reduce(jnp.add, [w * st_acc[i] for w, i in zip(ws, [u, *others])])
        st_m[u] = top
        st_l[u] = l
        st_acc[u] = acc

    def first(dyhi):
        for dz in range(Z):
            for r2 in range(2):
                k = lax.bitwise_xor(group, dyhi * Z + dz) * 4 + 2 * half + r2
                extra = bias[jnp.minimum(cnt[k], 4)]
                store_partial(unit_of(dyhi, dz, r2), queries_of(dyhi, dz, r2), tiles_of(k, 0), extra)

    def beyond(which):
        count = nover[which]

        def four(i, _):
            units = []
            for j in range(4):
                at = i * 4 + j
                item = over[which * 32 + jnp.minimum(at, 31)]
                k, c = item // 4, item % 4
                apart = lax.bitwise_xor(group, k // 4)
                dyhi, dz, r2 = apart // Z, apart % Z, k % 2
                extra = bias[jnp.where(at < count, jnp.clip(cnt[k] - c * 4, 0, 4), 0)]
                store_partial(spare + j, queries_of(dyhi, dz, r2), tiles_of(k, c * 4), extra)
                units.append(unit_of(dyhi, dz, r2))
            for j in range(4):
                merge(units[j], [spare + j])
            return 0

        lax.fori_loop(0, (count + 3) // 4, four, 0)

    def resident():
        for r2 in range(2):
            r = 2 * half + r2
            here = jnp.clip(scal[2 + r] - ctx * 512, 0, 512)
            q = queries_of(0, 0, r2)
            for c in range(8):
                limit = jnp.where(lane < (here - c * 64) * 4, bias[4], NONE)
                store_partial(spare + r2 * 8 + c, q, cache[r, c * 256 : (c + 1) * 256, :], limit)
        for r2 in range(2):
            merge(unit_of(0, 0, r2), [spare + r2 * 8 + c for c in range(8)])

    def finish(dyhi):
        row, lane = iota((128, 128), 0) % 32, iota((128, 128), 1)
        for pair in range(Z // 2):
            total = jnp.zeros((4, 128), f32)
            for j in range(4):
                dz, r2 = 2 * pair + j // 2, j % 2
                u = unit_of(dyhi, dz, r2)
                l = st_l[u]
                o = (st_acc[u] / l).astype(bf16)
                lse = jnp.where(lane == row + 32 * j, st_m[u] + jnp.log2(l), 0.0)
                total = total + jnp.sum(lse.reshape(4, 32, 128), axis=1)
                for t, (i, rows) in enumerate(places(dyhi, dz, r2)):
                    outs[i][rows, :] = o[t * 32 : (t + 1) * 32]
            for t in range(4):
                if half:
                    kept[t // 2, pl.ds((2 * dyhi + t % 2) * 4 + pair, 1), :] = total[t : t + 1]
                else:
                    kept[0, pl.ds(t * 4 + pair, 1), :] = total[t : t + 1]

    def per_group_half(work):
        if half:
            lax.fori_loop(0, 2, lambda dyhi, _: (work(dyhi), 0)[1], 0)
        else:
            work(d // 2)

    per_group_half(first)
    if half:
        beyond(1)
        beyond(3)
        resident()
    else:
        beyond(lax.bitwise_xor(group // Z, d // 2) * 2)
        if d < 2:
            resident()
    per_group_half(finish)
    for i in range(n):
        for j, part in enumerate(split3(kept[i])):
            outs[i][2048 + 16 * j : 2064 + 16 * j, :] = part


def shares(lses):
    top = functools.reduce(jnp.maximum, lses)
    parts = [jnp.exp2(l - top) for l in lses]
    total = functools.reduce(jnp.add, parts)
    return [p / total for p in parts], top + jnp.log2(total)


def mixed(weights, tiles):
    eye = iota((128, 128), 0) == iota((128, 128), 1)
    scales = jnp.concatenate([jnp.where(eye, w, 0.0).astype(bf16) for w in weights], axis=1)
    return jnp.dot(scales, jnp.concatenate(tiles, axis=0), preferred_element_type=f32)


def lse_of(ref, n):
    tail = ref[128 * n :, :].astype(f32)
    return tail[0:n] + tail[n : 2 * n] + tail[2 * n : 3 * n]


def put_lse(ref, lse):
    n = lse.shape[0]
    rows = [p.astype(f32) for p in split3(lse)]
    rows.append(jnp.zeros((16 - 3 * n, 128), f32))
    ref[128 * n :, :] = jnp.concatenate(rows, axis=0).astype(bf16)


def merged(ins, n):
    weights, lse = shares([lse_of(ref, n) for ref in ins])
    outs = []
    for p in range(n):
        o = mixed([w[p : p + 1] for w in weights], [ref[p * 128 : (p + 1) * 128, :] for ref in ins])
        outs.append(o.astype(bf16))
    return outs, lse


def put(outs, tiles, lse):
    n = len(tiles) // len(outs)
    for i, out in enumerate(outs):
        for j in range(n):
            out[j * 128 : (j + 1) * 128, :] = tiles[i * n + j]
        put_lse(out, lse[i * n : (i + 1) * n])


def plane_kernel(*refs):
    for half in range(2):
        put(refs[8 + 4 * half : 12 + 4 * half], *merged(refs[4 * half : 4 * half + 4], 16))


def line_kernel(*refs):
    left = iota((4, 128), 1) < 64
    (a, lse_a), (b, lse_b) = merged(refs[:4], 4), merged(refs[4:8], 4)

    def turned(lse):
        return pltpu.roll(jnp.concatenate([lse, lse], axis=0), 64, 1)[0:4]

    even = jnp.where(left, lse_a, turned(lse_b))
    odd = jnp.where(left, turned(lse_a), lse_b)
    tiles, rows = [], []
    for p in range(4):
        for i, lse in ((0, even), (1, odd)):
            half = slice(64 * i, 64 * i + 64)
            tiles.append(jnp.concatenate([a[p][half], b[p][half]], axis=0))
            rows.append(lse[p : p + 1])
    order = (0, 4, 2, 6, 1, 5, 3, 7)
    put(refs[8:10], [tiles[i] for i in order], jnp.concatenate([rows[i] for i in order], axis=0))


def halve_kernel(n, one, two, low, high):
    put((low, high), *merged((one, two), n))


def last_kernel(one, two, o_fresh, lse_fresh, out):
    weights, _ = shares([lse_of(one, 1), lse_of(two, 1), lse_fresh[0:1, :]])
    out[...] = mixed(weights, [one[0:128, :], two[0:128, :], o_fresh[...]]).astype(bf16)


def call(kernel, outs, ins, scratch=(), specs=None, out_specs=None, flops=0, size=0):
    shapes = [jax.ShapeDtypeStruct(s, d) for s, d in outs]
    return pl.pallas_call(
        kernel,
        out_shape=shapes,
        in_specs=specs or [VMEM] * len(ins),
        out_specs=out_specs or [VMEM] * len(outs),
        scratch_shapes=list(scratch),
        compiler_params=pltpu.CompilerParams(vmem_limit_bytes=40 << 20),
        cost_estimate=pl.CostEstimate(flops=flops, bytes_accessed=size, transcendentals=0),
    )(*ins)


def body(queries, fresh_key_value, key_value_cache, lens, blocks, block_group, block_request):
    ctx, grp, head = (lax.axis_index(a) for a in ("ctx", "grp", "head"))
    pair = [(0, 1), (1, 0)]
    tie = lax.optimization_barrier
    q = queries.reshape(4, 16, 2, 128).transpose(0, 2, 1, 3).reshape(2, 1, 1, 1, 64, 128)

    q, blocks, key_value_cache = tie((q, blocks, key_value_cache))
    line = jnp.concatenate([q, swapped(q, dz=4)], axis=1)
    other = lax.dynamic_slice_in_dim(blocks, 4 - 4 * head, 4, 2).reshape(64, 64, 256)
    line, other, blocks, key_value_cache = tie((line, other, blocks, key_value_cache))
    line = jnp.concatenate([line, swapped(line, dz=2)], axis=2)
    mine = lax.dynamic_slice_in_dim(blocks, 4 * head, 4, 2).reshape(64, 64, 256)
    theirs = lax.ppermute(other, "head", pair)
    line, mine, key_value_cache = tie((line, mine, key_value_cache))
    line = jnp.concatenate([line, swapped(line, dz=1)], axis=3)
    cache = key_value_cache.reshape(4, 2048, 256)
    line, cache = tie((line, cache))
    line_a, line_b = line[0].reshape(512, 128), line[1].reshape(512, 128)
    plane_a = jnp.concatenate([line_a] + [swapped(line_a, dx=d) for d in (1, 2, 3)], axis=0)
    plane_b = jnp.concatenate([line_b] + [swapped(line_b, dy=d) for d in (1, 2, 3)], axis=0)
    qa, qb = {0: plane_a}, {0: plane_b}
    for d in (1, 3, 2):
        qa[d] = swapped(plane_a, dy=d)
        qb[d] = swapped(plane_b, dx=d)

    key = block_group[:, 0] * 4 + block_request
    blk = jnp.concatenate([mine, theirs], axis=0)
    keys = jnp.concatenate([key, lax.ppermute(key, "head", pair)], axis=0)
    scal = jnp.concatenate([jnp.stack([grp, ctx]).astype(jnp.int32), lens[0]])
    lists = call(
        index_kernel,
        [((1024,), jnp.int32), ((64,), jnp.int32), ((128,), jnp.int32), ((4,), jnp.int32)],
        [keys],
        specs=[SMEM],
        out_specs=[SMEM] * 4,
    )
    o_fresh, lse_fresh = call(
        fresh_kernel, [((128, 128), bf16), ((8, 128), f32)], [q.reshape(128, 128), fresh_key_value.reshape(64, 256)]
    )

    def piece(half, d, q_in):
        n = 1 + half
        return call(
            functools.partial(piece_kernel, half, d),
            [((2096, 128), bf16)] * n,
            [scal, *lists, *q_in, blk, cache],
            scratch=[pltpu.VMEM((5, 8, 256), f32)]
            + [pltpu.VMEM((16 * n + 16, 128, 128), f32)] * 3
            + [pltpu.VMEM((n, 16, 128), f32)],
            specs=[SMEM] * 5 + [VMEM] * (n + 2),
            flops=6 << 30,
            size=10 << 20,
        )

    pa, pb = {}, {}
    for half, d in ((0, 1), (1, 1), (0, 3), (1, 0), (0, 2), (0, 0)):
        if half:
            one, two = (1, 3) if d else (0, 2)
            pb[one], pb[two] = piece(1, d, [qb[one], qb[two]])
        else:
            (pa[d],) = piece(0, d, [qa[d]])
    for d in (1, 3, 2):
        pa[d], pb[d] = swapped(pa[d], dy=d), swapped(pb[d], dx=d)
    lines = call(
        plane_kernel, [((528, 128), bf16)] * 8, [pa[d] for d in range(4)] + [pb[d] for d in range(4)], size=6 << 20
    )
    ca = [lines[0]] + [swapped(lines[d], dx=d) for d in (1, 2, 3)]
    cb = [lines[4]] + [swapped(lines[4 + d], dy=d) for d in (1, 2, 3)]
    low, high = call(line_kernel, [((528, 128), bf16)] * 2, [*ca, *cb], size=2 << 20)
    low, high = call(functools.partial(halve_kernel, 4), [((272, 128), bf16)] * 2, [low, swapped(high, dz=1)])
    low, high = call(functools.partial(halve_kernel, 2), [((144, 128), bf16)] * 2, [low, swapped(high, dz=2)])
    (out,) = call(last_kernel, [((128, 128), bf16)], [low, swapped(high, dz=4), o_fresh, lse_fresh])
    return out.reshape(4, 2, 16, 128).transpose(0, 2, 1, 3).reshape(queries.shape)


def solution(mesh):
    return jax.shard_map(
        body,
        mesh=mesh,
        in_specs=(
            P("grp", None, None, "head", "ctx"),
            P("grp", None, None, "head", None),
            P("grp", None, "ctx", "head", None),
            P("grp", None),
            P(("ctx", "grp", "head"), None, None, None),
            P(("ctx", "grp", "head"), None),
            P(("ctx", "grp", "head")),
        ),
        out_specs=P("grp", None, None, "head", "ctx"),
        check_vma=False,
    )
```

```python
import functools

import jax
import jax.numpy as jnp
from jax import lax
from jax.experimental import pallas as pl
from jax.experimental.pallas import tpu as pltpu
from jax.sharding import PartitionSpec as P

NONE = -1e30
X, Y, Z = 4, 4, 8
LOG2E = 1.4426950408889634
CNT, OVER, NOVER, SCAL, TABLE = 1024, 1088, 1216, 1220, 1280
VMEM = pl.BlockSpec(memory_space=pltpu.VMEM)
SMEM = pl.BlockSpec(memory_space=pltpu.SMEM)
bf16, f32 = jnp.bfloat16, jnp.float32


def place(x, y, z):
    return ((y % 2) * X + x) * (2 * Z) + (y // 2) * Z + z


def swapped(value, dx=0, dy=0, dz=0):
    route = [
        (place(x, y, z), place(x ^ dx, y ^ dy, z ^ dz))
        for x in range(X)
        for y in range(Y)
        for z in range(Z)
    ]
    return lax.ppermute(value, ("ctx", "grp"), route)


def iota(shape, dim):
    return lax.broadcasted_iota(jnp.int32, shape, dim)


def split3(value):
    high = value.astype(bf16)
    rest = value - high.astype(f32)
    middle = rest.astype(bf16)
    low = (rest - middle.astype(f32)).astype(bf16)
    return high, middle, low


def scores(q, k):
    return lax.dot_general(q, k, (((1,), (1,)), ((), ())), preferred_element_type=f32)


def fresh_kernel(q_ref, kv_ref, o_ref, lse_ref):
    s = scores(q_ref[...], kv_ref[:, :128]) * (128**-0.5 * LOG2E)
    row, col = iota(s.shape, 0), iota(s.shape, 1)
    valid = (row // 32 == col // 16) & (row % 4 == col % 4) & ((col % 16) // 4 <= (row % 16) // 4)
    s = jnp.where(valid, s, NONE)
    m = jnp.max(s, axis=1, keepdims=True)
    p = jnp.exp2(s - m)
    l = jnp.sum(p, axis=1, keepdims=True)
    acc = jnp.dot(p.astype(bf16), kv_ref[:, 128:], preferred_element_type=f32)
    o_ref[...] = (acc / l).astype(bf16)
    lse = jnp.broadcast_to(m + jnp.log2(l), (128, 128))
    eye = iota((128, 128), 0) == iota((128, 128), 1)
    lse_ref[...] = jnp.broadcast_to(jnp.sum(jnp.where(eye, lse, 0.0), axis=0, keepdims=True), (8, 128))


def split_kernel(scal, blocks, mine, other):
    row, lane = iota((128, 128), 0), iota((128, 128), 1)
    first = 4 * scal[2]
    start = jnp.where(row < 64, first, 4 - first)
    at = row % 64
    select = jnp.where(lane == (at // 4) * 8 + start + at % 4, 1.0, 0.0).astype(bf16)

    def eight(i, _):
        for j in range(8):
            b = i * 8 + j
            both = jnp.dot(select, blocks[b], preferred_element_type=f32).astype(bf16)
            mine[b] = both[:64]
            other[b] = both[64:]
        return 0

    lax.fori_loop(0, 8, eight, 0)


def index_kernel(scal, keys, table):
    for i in range(7):
        table[SCAL + i] = scal[i]

    def clear(i, _):
        table[CNT + i] = 0
        for j in range(16):
            table[i * 16 + j] = 0
        table[OVER + 2 * i] = 0
        table[OVER + 2 * i + 1] = 0
        return 0

    lax.fori_loop(0, 64, clear, 0)
    for i in range(4):
        table[NOVER + i] = 0

    def enter(i, _):
        k = keys[i]
        c = table[CNT + k]
        table[k * 16 + jnp.minimum(c, 15)] = i
        table[CNT + k] = c + 1

        @pl.when((c % 4 == 0) & (c > 0) & (c < 16))
        def _():
            which = (k // 32) * 2 + (k % 4) // 2
            n = table[NOVER + which]
            table[OVER + which * 32 + jnp.minimum(n, 31)] = k * 4 + c // 4
            table[NOVER + which] = n + 1

        return 0

    lax.fori_loop(0, 128, enter, 0)


def piece_kernel(half, d, table, *refs):
    n = 1 + half
    q_refs, (blk, cache), outs = refs[:n], refs[n : n + 2], refs[n + 2 : 2 * n + 2]
    bias, st_m, st_l, st_acc, kept = refs[2 * n + 2 :]
    scale = 128**-0.5 * LOG2E
    group, ctx = table[SCAL], table[SCAL + 1]
    row, lane = iota((8, 256), 0), iota((8, 256), 1)
    for i in range(5):
        bias[i] = jnp.where((row % 4 == lane % 4) & (lane < i * 64), 0.0, NONE)
    ones = jnp.ones((256, 128), bf16)
    unit_count = 16 * n
    spare = unit_count

    def places(dyhi, dz, r2):
        if half:
            slots = [(i, (2 * dyhi + dylo) * Z + dz) for i in range(2) for dylo in range(2)]
        else:
            slots = [(0, dx * Z + dz) for dx in range(X)]
        return [(i, pl.ds(pl.multiple_of(s * 64 + r2 * 32, 32), 32)) for i, s in slots]

    def queries_of(dyhi, dz, r2):
        return jnp.concatenate([q_refs[i][rows, :] for i, rows in places(dyhi, dz, r2)], axis=0)

    def unit_of(dyhi, dz, r2):
        return (dyhi * Z + dz) * 2 + r2 if half else dz * 2 + r2

    def tiles_of(k, start):
        return jnp.concatenate([blk[table[k * 16 + start + j]] for j in range(4)], axis=0)

    def store_partial(u, q, kv, extra):
        s = scores(q, kv[:, :128])
        s = (s.reshape(16, 8, 256) * scale + extra[None]).reshape(128, 256)
        m = jnp.max(s, axis=1, keepdims=True)
        p = jnp.exp2(s - m).astype(bf16)
        both = jnp.dot(p, jnp.concatenate([ones, kv[:, 128:]], axis=1), preferred_element_type=f32)
        st_m[u] = jnp.broadcast_to(m, (128, 128))
        st_l[u] = both[:, :128]
        st_acc[u] = both[:, 128:]

    def merge(u, others):
        ms = [st_m[i] for i in [u, *others]]
        top = functools.reduce(jnp.maximum, ms)
        ws = [jnp.exp2(m - top) for m in ms]
        l = functools.reduce(jnp.add, [w * st_l[i] for w, i in zip(ws, [u, *others])])
        acc = functools.reduce(jnp.add, [w * st_acc[i] for w, i in zip(ws, [u, *others])])
        st_m[u] = top
        st_l[u] = l
        st_acc[u] = acc

    def first(dyhi):
        for dz in range(Z):
            for r2 in range(2):
                k = lax.bitwise_xor(group, dyhi * Z + dz) * 4 + 2 * half + r2
                extra = bias[jnp.minimum(table[CNT + k], 4)]
                store_partial(unit_of(dyhi, dz, r2), queries_of(dyhi, dz, r2), tiles_of(k, 0), extra)

    def beyond(which):
        count = table[NOVER + which]

        def four(i, _):
            units = []
            for j in range(4):
                at = i * 4 + j
                item = table[OVER + which * 32 + jnp.minimum(at, 31)]
                k, c = item // 4, item % 4
                apart = lax.bitwise_xor(group, k // 4)
                dyhi, dz, r2 = apart // Z, apart % Z, k % 2
                extra = bias[jnp.where(at < count, jnp.clip(table[CNT + k] - c * 4, 0, 4), 0)]
                store_partial(spare + j, queries_of(dyhi, dz, r2), tiles_of(k, c * 4), extra)
                units.append(unit_of(dyhi, dz, r2))
            for j in range(4):
                merge(units[j], [spare + j])
            return 0

        lax.fori_loop(0, (count + 3) // 4, four, 0)

    def resident():
        for r2 in range(2):
            r = 2 * half + r2
            here = jnp.clip(table[SCAL + 3 + r] - ctx * 512, 0, 512)
            q = queries_of(0, 0, r2)
            for c in range(8):
                limit = jnp.where(lane < (here - c * 64) * 4, bias[4], NONE)
                store_partial(spare + r2 * 8 + c, q, cache[r, c * 256 : (c + 1) * 256, :], limit)
        for r2 in range(2):
            merge(unit_of(0, 0, r2), [spare + r2 * 8 + c for c in range(8)])

    def finish(dyhi):
        row, lane = iota((128, 128), 0) % 32, iota((128, 128), 1)
        for pair in range(Z // 2):
            total = jnp.zeros((4, 128), f32)
            for j in range(4):
                dz, r2 = 2 * pair + j // 2, j % 2
                u = unit_of(dyhi, dz, r2)
                l = st_l[u]
                o = (st_acc[u] / l).astype(bf16)
                lse = jnp.where(lane == row + 32 * j, st_m[u] + jnp.log2(l), 0.0)
                total = total + jnp.sum(lse.reshape(4, 32, 128), axis=1)
                for t, (i, rows) in enumerate(places(dyhi, dz, r2)):
                    outs[i][rows, :] = o[t * 32 : (t + 1) * 32]
            for t in range(4):
                if half:
                    kept[t // 2, pl.ds((2 * dyhi + t % 2) * 4 + pair, 1), :] = total[t : t + 1]
                else:
                    kept[0, pl.ds(t * 4 + pair, 1), :] = total[t : t + 1]

    def per_group_half(work):
        if half:
            lax.fori_loop(0, 2, lambda dyhi, _: (work(dyhi), 0)[1], 0)
        else:
            work(d // 2)

    per_group_half(first)
    if half:
        beyond(1)
        beyond(3)
        resident()
    else:
        beyond(lax.bitwise_xor(group // Z, d // 2) * 2)
        if d < 2:
            resident()
    per_group_half(finish)
    for i in range(n):
        for j, part in enumerate(split3(kept[i])):
            outs[i][2048 + 16 * j : 2064 + 16 * j, :] = part


def shares(lses):
    top = functools.reduce(jnp.maximum, lses)
    parts = [jnp.exp2(l - top) for l in lses]
    total = functools.reduce(jnp.add, parts)
    return [p / total for p in parts], top + jnp.log2(total)


def mixed(weights, tiles):
    eye = iota((128, 128), 0) == iota((128, 128), 1)
    scales = jnp.concatenate([jnp.where(eye, w, 0.0).astype(bf16) for w in weights], axis=1)
    return jnp.dot(scales, jnp.concatenate(tiles, axis=0), preferred_element_type=f32)


def lse_of(ref, n):
    tail = ref[128 * n :, :].astype(f32)
    return tail[0:n] + tail[n : 2 * n] + tail[2 * n : 3 * n]


def put_lse(ref, lse):
    n = lse.shape[0]
    rows = [p.astype(f32) for p in split3(lse)]
    rows.append(jnp.zeros((16 - 3 * n, 128), f32))
    ref[128 * n :, :] = jnp.concatenate(rows, axis=0).astype(bf16)


def merged(ins, n):
    weights, lse = shares([lse_of(ref, n) for ref in ins])
    outs = []
    for p in range(n):
        o = mixed([w[p : p + 1] for w in weights], [ref[p * 128 : (p + 1) * 128, :] for ref in ins])
        outs.append(o.astype(bf16))
    return outs, lse


def put(outs, tiles, lse):
    n = len(tiles) // len(outs)
    for i, out in enumerate(outs):
        for j in range(n):
            out[j * 128 : (j + 1) * 128, :] = tiles[i * n + j]
        put_lse(out, lse[i * n : (i + 1) * n])


def plane_kernel(*refs):
    put(refs[4:8], *merged(refs[:4], 16))


def line_kernel(*refs):
    left = iota((4, 128), 1) < 64
    (a, lse_a), (b, lse_b) = merged(refs[:4], 4), merged(refs[4:8], 4)

    def turned(lse):
        return pltpu.roll(jnp.concatenate([lse, lse], axis=0), 64, 1)[0:4]

    even = jnp.where(left, lse_a, turned(lse_b))
    odd = jnp.where(left, turned(lse_a), lse_b)
    tiles, rows = [], []
    for p in range(4):
        for i, lse in ((0, even), (1, odd)):
            half = slice(64 * i, 64 * i + 64)
            tiles.append(jnp.concatenate([a[p][half], b[p][half]], axis=0))
            rows.append(lse[p : p + 1])
    order = (0, 4, 2, 6, 1, 5, 3, 7)
    put(refs[8:10], [tiles[i] for i in order], jnp.concatenate([rows[i] for i in order], axis=0))


def halve_kernel(n, one, two, low, high):
    put((low, high), *merged((one, two), n))


def last_kernel(one, two, o_fresh, lse_fresh, out):
    weights, _ = shares([lse_of(one, 1), lse_of(two, 1), lse_fresh[0:1, :]])
    out[...] = mixed(weights, [one[0:128, :], two[0:128, :], o_fresh[...]]).astype(bf16)


def call(kernel, outs, ins, scratch=(), specs=None, out_specs=None, flops=0, size=0):
    shapes = [jax.ShapeDtypeStruct(s, d) for s, d in outs]
    return pl.pallas_call(
        kernel,
        out_shape=shapes,
        in_specs=specs or [VMEM] * len(ins),
        out_specs=out_specs or [VMEM] * len(outs),
        scratch_shapes=list(scratch),
        compiler_params=pltpu.CompilerParams(vmem_limit_bytes=40 << 20),
        cost_estimate=pl.CostEstimate(flops=flops, bytes_accessed=size, transcendentals=0),
    )(*ins)


def body(queries, fresh_key_value, key_value_cache, lens, blocks, block_group, block_request):
    ctx, grp, head = (lax.axis_index(a) for a in ("ctx", "grp", "head"))
    pair = [(0, 1), (1, 0)]
    tie = lax.optimization_barrier
    q = queries.reshape(4, 16, 2, 128).transpose(0, 2, 1, 3).reshape(2, 1, 1, 1, 64, 128)
    scal = jnp.concatenate([jnp.stack([grp, ctx, head]).astype(jnp.int32), lens[0]])
    key = block_group[:, 0] * 4 + block_request

    q, blocks, key_value_cache, key = tie((q, blocks, key_value_cache, key))
    line = jnp.concatenate([q, swapped(q, dz=4)], axis=1)
    mine, other = call(
        split_kernel,
        [((64, 64, 256), bf16)] * 2,
        [scal, blocks.reshape(64, 128, 256)],
        specs=[SMEM, VMEM],
        flops=1 << 30,
        size=8 << 20,
    )
    line, mine, other, key_value_cache, key = tie((line, mine, other, key_value_cache, key))
    line = jnp.concatenate([line, swapped(line, dz=2)], axis=2)
    theirs = lax.ppermute(other, "head", pair)
    keys = jnp.concatenate([key, lax.ppermute(key, "head", pair)], axis=0)
    line, keys, key_value_cache, q = tie((line, keys, key_value_cache, q))
    line = jnp.concatenate([line, swapped(line, dz=1)], axis=3)
    line, key_value_cache = tie((line, key_value_cache))
    line_a, line_b = line[0].reshape(512, 128), line[1].reshape(512, 128)
    plane_b = jnp.concatenate([line_b] + [swapped(line_b, dy=d) for d in (1, 2, 3)], axis=0)
    plane_a = jnp.concatenate([line_a] + [swapped(line_a, dx=d) for d in (1, 2, 3)], axis=0)
    cache = key_value_cache.reshape(4, 2048, 256)
    plane_a, plane_b, keys, mine, theirs = tie((plane_a, plane_b, keys, mine, theirs))
    qa, qb = {0: plane_a}, {0: plane_b}
    for d in (1, 3):
        qb[d] = swapped(plane_b, dx=d)
    for d in (1, 3):
        qa[d] = swapped(plane_a, dy=d)
    (table,) = call(
        index_kernel, [((TABLE,), jnp.int32)], [scal, keys], specs=[SMEM] * 2, out_specs=[SMEM], flops=4 << 30
    )
    blk = jnp.concatenate([mine, theirs], axis=0)
    o_fresh, lse_fresh = call(
        fresh_kernel, [((128, 128), bf16), ((8, 128), f32)], [q.reshape(128, 128), fresh_key_value.reshape(64, 256)]
    )
    plane_b, qb[1], qb[3] = tie((plane_b, qb[1], qb[3]))
    qb[2] = swapped(plane_b, dx=2)
    plane_a, qa[1], qa[3] = tie((plane_a, qa[1], qa[3]))
    qa[2] = swapped(plane_a, dy=2)

    def piece(half, d, q_in, table):
        n = 1 + half
        return call(
            functools.partial(piece_kernel, half, d),
            [((2096, 128), bf16)] * n,
            [table, *q_in, blk, cache],
            scratch=[pltpu.VMEM((5, 8, 256), f32)]
            + [pltpu.VMEM((16 * n + 16, 128, 128), f32)] * 3
            + [pltpu.VMEM((n, 16, 128), f32)],
            specs=[SMEM] + [VMEM] * (n + 2),
            flops=6 << 30,
            size=10 << 20,
        )

    pa, pb = {}, {}
    for half, d in ((1, 1), (0, 1), (0, 3), (1, 0), (0, 2), (0, 0)):
        if half:
            one, two = (1, 3) if d else (0, 2)
            pb[one], pb[two] = piece(1, d, [qb[one], qb[two]], table)
            pb[one], pb[two], table = tie((pb[one], pb[two], table))
            for i in (one, two):
                pb[i] = swapped(pb[i], dx=i) if i else pb[i]
        else:
            (pa[d],) = piece(0, d, [qa[d]], table)
            pa[d], table = tie((pa[d], table))
            pa[d] = swapped(pa[d], dy=d) if d else pa[d]
    planes = [((528, 128), bf16)] * 4
    ca = call(plane_kernel, planes, [pa[d] for d in range(4)], size=3 << 20)
    cb = call(plane_kernel, planes, [pb[d] for d in range(4)], size=3 << 20)
    ca = [ca[0]] + [swapped(ca[d], dx=d) for d in (1, 2, 3)]
    cb = [cb[0]] + [swapped(cb[d], dy=d) for d in (1, 2, 3)]
    low, high = call(line_kernel, [((528, 128), bf16)] * 2, [*ca, *cb], size=2 << 20)
    low, high = call(functools.partial(halve_kernel, 4), [((272, 128), bf16)] * 2, [low, swapped(high, dz=1)])
    low, high = call(functools.partial(halve_kernel, 2), [((144, 128), bf16)] * 2, [low, swapped(high, dz=2)])
    (out,) = call(last_kernel, [((128, 128), bf16)], [low, swapped(high, dz=4), o_fresh, lse_fresh])
    return out.reshape(4, 2, 16, 128).transpose(0, 2, 1, 3).reshape(queries.shape)


def solution(mesh):
    return jax.shard_map(
        body,
        mesh=mesh,
        in_specs=(
            P("grp", None, None, "head", "ctx"),
            P("grp", None, None, "head", None),
            P("grp", None, "ctx", "head", None),
            P("grp", None),
            P(("ctx", "grp", "head"), None, None, None),
            P(("ctx", "grp", "head"), None),
            P(("ctx", "grp", "head")),
        ),
        out_specs=P("grp", None, None, "head", "ctx"),
        check_vma=False,
    )
```

```python
import functools

import jax
import jax.numpy as jnp
from jax import lax
from jax.experimental import pallas as pl
from jax.experimental.pallas import tpu as pltpu
from jax.sharding import PartitionSpec as P

NONE = -1e30
X, Y, Z = 4, 4, 8
LOG2E = 1.4426950408889634
CNT, OVER, NOVER, SCAL, TABLE = 1024, 1088, 1216, 1220, 1280
VMEM = pl.BlockSpec(memory_space=pltpu.VMEM)
SMEM = pl.BlockSpec(memory_space=pltpu.SMEM)
bf16, f32 = jnp.bfloat16, jnp.float32


def place(x, y, z):
    return ((y % 2) * X + x) * (2 * Z) + (y // 2) * Z + z


def swapped(value, dx=0, dy=0, dz=0):
    route = [
        (place(x, y, z), place(x ^ dx, y ^ dy, z ^ dz))
        for x in range(X)
        for y in range(Y)
        for z in range(Z)
    ]
    return lax.ppermute(value, ("ctx", "grp"), route)


def iota(shape, dim):
    return lax.broadcasted_iota(jnp.int32, shape, dim)


def split3(value):
    high = value.astype(bf16)
    rest = value - high.astype(f32)
    middle = rest.astype(bf16)
    low = (rest - middle.astype(f32)).astype(bf16)
    return high, middle, low


def scores(q, k):
    return lax.dot_general(q, k, (((1,), (1,)), ((), ())), preferred_element_type=f32)


def fresh_kernel(q_ref, kv_ref, o_ref, lse_ref):
    s = scores(q_ref[...], kv_ref[:, :128]) * (128**-0.5 * LOG2E)
    row, col = iota(s.shape, 0), iota(s.shape, 1)
    valid = (row // 32 == col // 16) & (row % 4 == col % 4) & ((col % 16) // 4 <= (row % 16) // 4)
    s = jnp.where(valid, s, NONE)
    m = jnp.max(s, axis=1, keepdims=True)
    p = jnp.exp2(s - m)
    l = jnp.sum(p, axis=1, keepdims=True)
    acc = jnp.dot(p.astype(bf16), kv_ref[:, 128:], preferred_element_type=f32)
    o_ref[...] = (acc / l).astype(bf16)
    lse = jnp.broadcast_to(m + jnp.log2(l), (128, 128))
    eye = iota((128, 128), 0) == iota((128, 128), 1)
    lse_ref[...] = jnp.broadcast_to(jnp.sum(jnp.where(eye, lse, 0.0), axis=0, keepdims=True), (8, 128))


def split_kernel(scal, blocks, mine, other):
    row, lane = iota((128, 128), 0), iota((128, 128), 1)
    first = 4 * scal[2]
    start = jnp.where(row < 64, first, 4 - first)
    at = row % 64
    select = jnp.where(lane == (at // 4) * 8 + start + at % 4, 1.0, 0.0).astype(bf16)

    def eight(i, _):
        for j in range(8):
            b = i * 8 + j
            both = jnp.dot(select, blocks[b], preferred_element_type=f32).astype(bf16)
            mine[b] = both[:64]
            other[b] = both[64:]
        return 0

    lax.fori_loop(0, 8, eight, 0)


def cache_kernel(mixed_rows, cache):
    row, lane = iota((128, 128), 0), iota((128, 128), 1)
    at = row % 64
    select = jnp.where(lane == (at // 4) * 8 + (row // 64) * 4 + at % 4, 1.0, 0.0).astype(bf16)

    def sixteen(i, _):
        for j in range(16):
            b = i * 16 + j
            here = mixed_rows[pl.ds(pl.multiple_of(b * 128, 128), 128), :]
            both = jnp.dot(select, here, preferred_element_type=f32).astype(bf16)
            rows = pl.ds(pl.multiple_of(b * 64, 64), 64)
            cache[rows, :128] = both[:64]
            cache[rows, 128:] = both[64:]
        return 0

    lax.fori_loop(0, 8, sixteen, 0)


def index_kernel(scal, keys, table):
    for i in range(7):
        table[SCAL + i] = scal[i]

    def clear(i, _):
        table[CNT + i] = 0
        for j in range(16):
            table[i * 16 + j] = 0
        table[OVER + 2 * i] = 0
        table[OVER + 2 * i + 1] = 0
        return 0

    lax.fori_loop(0, 64, clear, 0)
    for i in range(4):
        table[NOVER + i] = 0

    def enter(i, _):
        k = keys[i]
        c = table[CNT + k]
        table[k * 16 + jnp.minimum(c, 15)] = i
        table[CNT + k] = c + 1

        @pl.when((c % 4 == 0) & (c > 0) & (c < 16))
        def _():
            which = (k // 32) * 2 + (k % 4) // 2
            n = table[NOVER + which]
            table[OVER + which * 32 + jnp.minimum(n, 31)] = k * 4 + c // 4
            table[NOVER + which] = n + 1

        return 0

    lax.fori_loop(0, 128, enter, 0)


def piece_kernel(half, d, table, *refs):
    n = 1 + half
    q_refs, (blk, cache), outs = refs[:n], refs[n : n + 2], refs[n + 2 : 2 * n + 2]
    bias, st_m, st_l, st_acc, kept = refs[2 * n + 2 :]
    scale = 128**-0.5 * LOG2E
    group, ctx = table[SCAL], table[SCAL + 1]
    row, lane = iota((8, 256), 0), iota((8, 256), 1)
    for i in range(5):
        bias[i] = jnp.where((row % 4 == lane % 4) & (lane < i * 64), 0.0, NONE)
    ones = jnp.ones((256, 128), bf16)
    unit_count = 16 * n
    spare = unit_count

    def places(dyhi, dz, r2):
        if half:
            slots = [(i, (2 * dyhi + dylo) * Z + dz) for i in range(2) for dylo in range(2)]
        else:
            slots = [(0, dx * Z + dz) for dx in range(X)]
        return [(i, pl.ds(pl.multiple_of(s * 64 + r2 * 32, 32), 32)) for i, s in slots]

    def queries_of(dyhi, dz, r2):
        return jnp.concatenate([q_refs[i][rows, :] for i, rows in places(dyhi, dz, r2)], axis=0)

    def unit_of(dyhi, dz, r2):
        return (dyhi * Z + dz) * 2 + r2 if half else dz * 2 + r2

    def tiles_of(k, start):
        return jnp.concatenate([blk[table[k * 16 + start + j]] for j in range(4)], axis=0)

    def store_partial(u, q, kv, extra):
        s = scores(q, kv[:, :128])
        s = (s.reshape(16, 8, 256) * scale + extra[None]).reshape(128, 256)
        m = jnp.max(s, axis=1, keepdims=True)
        p = jnp.exp2(s - m).astype(bf16)
        both = jnp.dot(p, jnp.concatenate([ones, kv[:, 128:]], axis=1), preferred_element_type=f32)
        st_m[u] = jnp.broadcast_to(m, (128, 128))
        st_l[u] = both[:, :128]
        st_acc[u] = both[:, 128:]

    def merge(u, others):
        ms = [st_m[i] for i in [u, *others]]
        top = functools.reduce(jnp.maximum, ms)
        ws = [jnp.exp2(m - top) for m in ms]
        l = functools.reduce(jnp.add, [w * st_l[i] for w, i in zip(ws, [u, *others])])
        acc = functools.reduce(jnp.add, [w * st_acc[i] for w, i in zip(ws, [u, *others])])
        st_m[u] = top
        st_l[u] = l
        st_acc[u] = acc

    def first(dyhi):
        for dz in range(Z):
            for r2 in range(2):
                k = lax.bitwise_xor(group, dyhi * Z + dz) * 4 + 2 * half + r2
                extra = bias[jnp.minimum(table[CNT + k], 4)]
                store_partial(unit_of(dyhi, dz, r2), queries_of(dyhi, dz, r2), tiles_of(k, 0), extra)

    def beyond(which):
        count = table[NOVER + which]

        def four(i, _):
            units = []
            for j in range(4):
                at = i * 4 + j
                item = table[OVER + which * 32 + jnp.minimum(at, 31)]
                k, c = item // 4, item % 4
                apart = lax.bitwise_xor(group, k // 4)
                dyhi, dz, r2 = apart // Z, apart % Z, k % 2
                extra = bias[jnp.where(at < count, jnp.clip(table[CNT + k] - c * 4, 0, 4), 0)]
                store_partial(spare + j, queries_of(dyhi, dz, r2), tiles_of(k, c * 4), extra)
                units.append(unit_of(dyhi, dz, r2))
            for j in range(4):
                merge(units[j], [spare + j])
            return 0

        lax.fori_loop(0, (count + 3) // 4, four, 0)

    def resident():
        for r2 in range(2):
            r = 2 * half + r2
            here = jnp.clip(table[SCAL + 3 + r] - ctx * 512, 0, 512)
            q = queries_of(0, 0, r2)
            for c in range(8):
                limit = jnp.where(lane < (here - c * 64) * 4, bias[4], NONE)
                store_partial(spare + r2 * 8 + c, q, cache[r, c * 256 : (c + 1) * 256, :], limit)
        for r2 in range(2):
            merge(unit_of(0, 0, r2), [spare + r2 * 8 + c for c in range(8)])

    def finish(dyhi):
        row, lane = iota((128, 128), 0) % 32, iota((128, 128), 1)
        for pair in range(Z // 2):
            total = jnp.zeros((4, 128), f32)
            for j in range(4):
                dz, r2 = 2 * pair + j // 2, j % 2
                u = unit_of(dyhi, dz, r2)
                l = st_l[u]
                o = (st_acc[u] / l).astype(bf16)
                lse = jnp.where(lane == row + 32 * j, st_m[u] + jnp.log2(l), 0.0)
                total = total + jnp.sum(lse.reshape(4, 32, 128), axis=1)
                for t, (i, rows) in enumerate(places(dyhi, dz, r2)):
                    outs[i][rows, :] = o[t * 32 : (t + 1) * 32]
            for t in range(4):
                if half:
                    kept[t // 2, pl.ds((2 * dyhi + t % 2) * 4 + pair, 1), :] = total[t : t + 1]
                else:
                    kept[0, pl.ds(t * 4 + pair, 1), :] = total[t : t + 1]

    def per_group_half(work):
        if half:
            lax.fori_loop(0, 2, lambda dyhi, _: (work(dyhi), 0)[1], 0)
        else:
            work(d // 2)

    per_group_half(first)
    if half:
        beyond(1)
        beyond(3)
        resident()
    else:
        beyond(lax.bitwise_xor(group // Z, d // 2) * 2)
        if d < 2:
            resident()
    per_group_half(finish)
    for i in range(n):
        for j, part in enumerate(split3(kept[i])):
            outs[i][2048 + 16 * j : 2064 + 16 * j, :] = part


def shares(lses):
    top = functools.reduce(jnp.maximum, lses)
    parts = [jnp.exp2(l - top) for l in lses]
    total = functools.reduce(jnp.add, parts)
    return [p / total for p in parts], top + jnp.log2(total)


def mixed(weights, tiles):
    eye = iota((128, 128), 0) == iota((128, 128), 1)
    scales = jnp.concatenate([jnp.where(eye, w, 0.0).astype(bf16) for w in weights], axis=1)
    return jnp.dot(scales, jnp.concatenate(tiles, axis=0), preferred_element_type=f32)


def lse_of(ref, n):
    tail = ref[128 * n :, :].astype(f32)
    return tail[0:n] + tail[n : 2 * n] + tail[2 * n : 3 * n]


def put_lse(ref, lse):
    n = lse.shape[0]
    rows = [p.astype(f32) for p in split3(lse)]
    rows.append(jnp.zeros((16 - 3 * n, 128), f32))
    ref[128 * n :, :] = jnp.concatenate(rows, axis=0).astype(bf16)


def merged(ins, n):
    weights, lse = shares([lse_of(ref, n) for ref in ins])
    outs = []
    for p in range(n):
        o = mixed([w[p : p + 1] for w in weights], [ref[p * 128 : (p + 1) * 128, :] for ref in ins])
        outs.append(o.astype(bf16))
    return outs, lse


def put(outs, tiles, lse):
    n = len(tiles) // len(outs)
    for i, out in enumerate(outs):
        for j in range(n):
            out[j * 128 : (j + 1) * 128, :] = tiles[i * n + j]
        put_lse(out, lse[i * n : (i + 1) * n])


def plane_kernel(*refs):
    put(refs[4:8], *merged(refs[:4], 16))


def line_kernel(*refs):
    left = iota((4, 128), 1) < 64
    (a, lse_a), (b, lse_b) = merged(refs[:4], 4), merged(refs[4:8], 4)

    def turned(lse):
        return pltpu.roll(jnp.concatenate([lse, lse], axis=0), 64, 1)[0:4]

    even = jnp.where(left, lse_a, turned(lse_b))
    odd = jnp.where(left, turned(lse_a), lse_b)
    tiles, rows = [], []
    for p in range(4):
        for i, lse in ((0, even), (1, odd)):
            half = slice(64 * i, 64 * i + 64)
            tiles.append(jnp.concatenate([a[p][half], b[p][half]], axis=0))
            rows.append(lse[p : p + 1])
    order = (0, 4, 2, 6, 1, 5, 3, 7)
    put(refs[8:10], [tiles[i] for i in order], jnp.concatenate([rows[i] for i in order], axis=0))


def halve_kernel(n, one, two, low, high):
    put((low, high), *merged((one, two), n))


def last_kernel(one, two, o_fresh, lse_fresh, out):
    weights, _ = shares([lse_of(one, 1), lse_of(two, 1), lse_fresh[0:1, :]])
    out[...] = mixed(weights, [one[0:128, :], two[0:128, :], o_fresh[...]]).astype(bf16)


def call(kernel, outs, ins, scratch=(), specs=None, out_specs=None, flops=0, size=0):
    shapes = [jax.ShapeDtypeStruct(s, d) for s, d in outs]
    return pl.pallas_call(
        kernel,
        out_shape=shapes,
        in_specs=specs or [VMEM] * len(ins),
        out_specs=out_specs or [VMEM] * len(outs),
        scratch_shapes=list(scratch),
        compiler_params=pltpu.CompilerParams(vmem_limit_bytes=40 << 20),
        cost_estimate=pl.CostEstimate(flops=flops, bytes_accessed=size, transcendentals=0),
    )(*ins)


def body(queries, fresh_key_value, key_value_cache, lens, blocks, block_group, block_request):
    ctx, grp, head = (lax.axis_index(a) for a in ("ctx", "grp", "head"))
    pair = [(0, 1), (1, 0)]
    tie = lax.optimization_barrier
    q = queries.reshape(4, 16, 2, 128).transpose(0, 2, 1, 3).reshape(2, 1, 1, 1, 64, 128)
    scal = jnp.concatenate([jnp.stack([grp, ctx, head]).astype(jnp.int32), lens[0]])
    key = block_group[:, 0] * 4 + block_request

    q, blocks, key_value_cache, key = tie((q, blocks, key_value_cache, key))
    line = jnp.concatenate([q, swapped(q, dz=4)], axis=1)
    mine, other = call(
        split_kernel,
        [((64, 64, 256), bf16)] * 2,
        [scal, blocks.reshape(64, 128, 256)],
        specs=[SMEM, VMEM],
        flops=1 << 30,
        size=8 << 20,
    )
    line, mine, other, key_value_cache, key = tie((line, mine, other, key_value_cache, key))
    line = jnp.concatenate([line, swapped(line, dz=2)], axis=2)
    theirs = lax.ppermute(other, "head", pair)
    keys = jnp.concatenate([key, lax.ppermute(key, "head", pair)], axis=0)
    line, keys, key_value_cache, q = tie((line, keys, key_value_cache, q))
    line = jnp.concatenate([line, swapped(line, dz=1)], axis=3)
    line, key_value_cache, theirs = tie((line, key_value_cache, theirs))
    line_a, line_b = line[0].reshape(512, 128), line[1].reshape(512, 128)
    plane_b = jnp.concatenate([line_b] + [swapped(line_b, dy=d) for d in (1, 2, 3)], axis=0)
    plane_a = jnp.concatenate([line_a] + [swapped(line_a, dx=d) for d in (1, 2, 3)], axis=0)
    rows = key_value_cache.reshape(4, 512, 4, 2, 128).transpose(0, 1, 3, 2, 4).reshape(16384, 128)
    (cache,) = call(cache_kernel, [((8192, 256), bf16)], [rows], size=8 << 20)
    cache = cache.reshape(4, 2048, 256)
    plane_a, plane_b, keys, mine, theirs = tie((plane_a, plane_b, keys, mine, theirs))
    qa, qb = {0: plane_a}, {0: plane_b}
    for d in (1, 3):
        qb[d] = swapped(plane_b, dx=d)
    for d in (1, 3):
        qa[d] = swapped(plane_a, dy=d)
    (table,) = call(
        index_kernel, [((TABLE,), jnp.int32)], [scal, keys], specs=[SMEM] * 2, out_specs=[SMEM], flops=4 << 30
    )
    blk = jnp.concatenate([mine, theirs], axis=0)
    o_fresh, lse_fresh = call(
        fresh_kernel, [((128, 128), bf16), ((8, 128), f32)], [q.reshape(128, 128), fresh_key_value.reshape(64, 256)]
    )
    plane_b, qb[1], qb[3] = tie((plane_b, qb[1], qb[3]))
    qb[2] = swapped(plane_b, dx=2)
    plane_a, qa[1], qa[3] = tie((plane_a, qa[1], qa[3]))
    qa[2] = swapped(plane_a, dy=2)

    def piece(half, d, q_in, table):
        n = 1 + half
        return call(
            functools.partial(piece_kernel, half, d),
            [((2096, 128), bf16)] * n,
            [table, *q_in, blk, cache],
            scratch=[pltpu.VMEM((5, 8, 256), f32)]
            + [pltpu.VMEM((16 * n + 16, 128, 128), f32)] * 3
            + [pltpu.VMEM((n, 16, 128), f32)],
            specs=[SMEM] + [VMEM] * (n + 2),
            flops=8 << 28,
            size=10 << 20,
        )

    pa, pb = {}, {}
    for half, d in ((0, 0), (1, 1), (0, 1), (0, 3), (1, 0), (0, 2)):
        if half:
            one, two = (1, 3) if d else (0, 2)
            if not d:
                pb[1], pb[3], table = tie((pb[1], pb[3], table))
            pb[one], pb[two] = piece(1, d, [qb[one], qb[two]], table)
            pb[one], pb[two], table = tie((pb[one], pb[two], table))
            for i in (one, two):
                pb[i] = swapped(pb[i], dx=i) if i else pb[i]
        else:
            (pa[d],) = piece(0, d, [qa[d]], table)
            pa[d], table = tie((pa[d], table))
            pa[d] = swapped(pa[d], dy=d) if d else pa[d]
    planes = [((528, 128), bf16)] * 4
    ca = call(plane_kernel, planes, [pa[d] for d in range(4)], size=3 << 20)
    cb = call(plane_kernel, planes, [pb[d] for d in range(4)], size=3 << 20)
    ca = [ca[0]] + [swapped(ca[d], dx=d) for d in (1, 2, 3)]
    cb = [cb[0]] + [swapped(cb[d], dy=d) for d in (1, 2, 3)]
    low, high = call(line_kernel, [((528, 128), bf16)] * 2, [*ca, *cb], size=2 << 20)
    low, high = call(functools.partial(halve_kernel, 4), [((272, 128), bf16)] * 2, [low, swapped(high, dz=1)])
    low, high = call(functools.partial(halve_kernel, 2), [((144, 128), bf16)] * 2, [low, swapped(high, dz=2)])
    (out,) = call(last_kernel, [((128, 128), bf16)], [low, swapped(high, dz=4), o_fresh, lse_fresh])
    return out.reshape(4, 2, 16, 128).transpose(0, 2, 1, 3).reshape(queries.shape)


def solution(mesh):
    return jax.shard_map(
        body,
        mesh=mesh,
        in_specs=(
            P("grp", None, None, "head", "ctx"),
            P("grp", None, None, "head", None),
            P("grp", None, "ctx", "head", None),
            P("grp", None),
            P(("ctx", "grp", "head"), None, None, None),
            P(("ctx", "grp", "head"), None),
            P(("ctx", "grp", "head")),
        ),
        out_specs=P("grp", None, None, "head", "ctx"),
        check_vma=False,
    )
```

```python
import functools

import jax
import jax.numpy as jnp
from jax import lax
from jax.experimental import pallas as pl
from jax.experimental.pallas import tpu as pltpu
from jax.sharding import PartitionSpec as P

NONE = -1e30
X, Y, Z = 4, 4, 8
LOG2E = 1.4426950408889634
CNT, OVER, NOVER, SCAL, TABLE = 1024, 1088, 1216, 1220, 1280
VMEM = pl.BlockSpec(memory_space=pltpu.VMEM)
SMEM = pl.BlockSpec(memory_space=pltpu.SMEM)
bf16, f32 = jnp.bfloat16, jnp.float32


def place(x, y, z):
    return ((y % 2) * X + x) * (2 * Z) + (y // 2) * Z + z


def swapped(value, dx=0, dy=0, dz=0):
    route = [
        (place(x, y, z), place(x ^ dx, y ^ dy, z ^ dz))
        for x in range(X)
        for y in range(Y)
        for z in range(Z)
    ]
    return lax.ppermute(value, ("ctx", "grp"), route)


def iota(shape, dim):
    return lax.broadcasted_iota(jnp.int32, shape, dim)


def split3(value):
    high = value.astype(bf16)
    rest = value - high.astype(f32)
    middle = rest.astype(bf16)
    low = (rest - middle.astype(f32)).astype(bf16)
    return high, middle, low


def scores(q, k):
    return lax.dot_general(q, k, (((1,), (1,)), ((), ())), preferred_element_type=f32)


def fresh_kernel(q_ref, kv_ref, o_ref, lse_ref):
    s = scores(q_ref[...], kv_ref[:, :128]) * (128**-0.5 * LOG2E)
    row, col = iota(s.shape, 0), iota(s.shape, 1)
    valid = (row // 32 == col // 16) & (row % 4 == col % 4) & ((col % 16) // 4 <= (row % 16) // 4)
    s = jnp.where(valid, s, NONE)
    m = jnp.max(s, axis=1, keepdims=True)
    p = jnp.exp2(s - m)
    l = jnp.sum(p, axis=1, keepdims=True)
    acc = jnp.dot(p.astype(bf16), kv_ref[:, 128:], preferred_element_type=f32)
    o_ref[...] = (acc / l).astype(bf16)
    lse = jnp.broadcast_to(m + jnp.log2(l), (128, 128))
    eye = iota((128, 128), 0) == iota((128, 128), 1)
    lse_ref[...] = jnp.broadcast_to(jnp.sum(jnp.where(eye, lse, 0.0), axis=0, keepdims=True), (8, 128))


def split_kernel(scal, blocks, mine, other):
    row, lane = iota((128, 128), 0), iota((128, 128), 1)
    first = 4 * scal[2]
    start = jnp.where(row < 64, first, 4 - first)
    at = row % 64
    select = jnp.where(lane == (at // 4) * 8 + start + at % 4, 1.0, 0.0).astype(bf16)

    def eight(i, _):
        for j in range(8):
            b = i * 8 + j
            both = jnp.dot(select, blocks[b], preferred_element_type=f32).astype(bf16)
            mine[b] = both[:64]
            other[b] = both[64:]
        return 0

    lax.fori_loop(0, 8, eight, 0)


def cache_kernel(mixed_rows, cache):
    row, lane = iota((128, 128), 0), iota((128, 128), 1)
    at = row % 64
    select = jnp.where(lane == (at // 4) * 8 + (row // 64) * 4 + at % 4, 1.0, 0.0).astype(bf16)

    def sixteen(i, _):
        for j in range(16):
            b = i * 16 + j
            here = mixed_rows[pl.ds(pl.multiple_of(b * 128, 128), 128), :]
            both = jnp.dot(select, here, preferred_element_type=f32).astype(bf16)
            rows = pl.ds(pl.multiple_of(b * 64, 64), 64)
            cache[rows, :128] = both[:64]
            cache[rows, 128:] = both[64:]
        return 0

    lax.fori_loop(0, 8, sixteen, 0)


def index_kernel(scal, keys, table):
    for i in range(7):
        table[SCAL + i] = scal[i]

    def clear(i, _):
        table[CNT + i] = 0
        for j in range(16):
            table[i * 16 + j] = 0
        table[OVER + 2 * i] = 0
        table[OVER + 2 * i + 1] = 0
        return 0

    lax.fori_loop(0, 64, clear, 0)
    for i in range(4):
        table[NOVER + i] = 0

    def enter(i, _):
        k = keys[i]
        c = table[CNT + k]
        table[k * 16 + jnp.minimum(c, 15)] = i
        table[CNT + k] = c + 1

        @pl.when((c % 4 == 0) & (c > 0) & (c < 16))
        def _():
            which = (k // 32) * 2 + (k % 4) // 2
            n = table[NOVER + which]
            table[OVER + which * 32 + jnp.minimum(n, 31)] = k * 4 + c // 4
            table[NOVER + which] = n + 1

        return 0

    lax.fori_loop(0, 128, enter, 0)


def piece_kernel(half, d, table, *refs):
    n = 1 + half
    q_refs, (blk, cache), outs = refs[:n], refs[n : n + 2], refs[n + 2 : 2 * n + 2]
    bias, st_m, st_l, st_acc, kept = refs[2 * n + 2 :]
    scale = 128**-0.5 * LOG2E
    group, ctx = table[SCAL], table[SCAL + 1]
    row, lane = iota((8, 256), 0), iota((8, 256), 1)
    for i in range(5):
        bias[i] = jnp.where((row % 4 == lane % 4) & (lane < i * 64), 0.0, NONE)
    ones = jnp.ones((256, 128), bf16)
    unit_count = 16 * n
    spare = unit_count

    def places(dyhi, dz, r2):
        if half:
            slots = [(i, (2 * dyhi + dylo) * Z + dz) for i in range(2) for dylo in range(2)]
        else:
            slots = [(0, dx * Z + dz) for dx in range(X)]
        return [(i, pl.ds(pl.multiple_of(s * 64 + r2 * 32, 32), 32)) for i, s in slots]

    def queries_of(dyhi, dz, r2):
        return jnp.concatenate([q_refs[i][rows, :] for i, rows in places(dyhi, dz, r2)], axis=0)

    def unit_of(dyhi, dz, r2):
        return (dyhi * Z + dz) * 2 + r2 if half else dz * 2 + r2

    def tiles_of(k, start):
        return jnp.concatenate([blk[table[k * 16 + start + j]] for j in range(4)], axis=0)

    def store_partial(u, q, kv, extra):
        s = scores(q, kv[:, :128])
        s = (s.reshape(16, 8, 256) * scale + extra[None]).reshape(128, 256)
        m = jnp.max(s, axis=1, keepdims=True)
        p = jnp.exp2(s - m).astype(bf16)
        both = jnp.dot(p, jnp.concatenate([ones, kv[:, 128:]], axis=1), preferred_element_type=f32)
        st_m[u] = jnp.broadcast_to(m, (128, 128))
        st_l[u] = both[:, :128]
        st_acc[u] = both[:, 128:]

    def merge(u, others):
        ms = [st_m[i] for i in [u, *others]]
        top = functools.reduce(jnp.maximum, ms)
        ws = [jnp.exp2(m - top) for m in ms]
        l = functools.reduce(jnp.add, [w * st_l[i] for w, i in zip(ws, [u, *others])])
        acc = functools.reduce(jnp.add, [w * st_acc[i] for w, i in zip(ws, [u, *others])])
        st_m[u] = top
        st_l[u] = l
        st_acc[u] = acc

    def first(dyhi):
        for dz in range(Z):
            for r2 in range(2):
                k = lax.bitwise_xor(group, dyhi * Z + dz) * 4 + 2 * half + r2
                extra = bias[jnp.minimum(table[CNT + k], 4)]
                store_partial(unit_of(dyhi, dz, r2), queries_of(dyhi, dz, r2), tiles_of(k, 0), extra)

    def beyond(which):
        count = table[NOVER + which]

        def four(i, _):
            units = []
            for j in range(4):
                at = i * 4 + j
                item = table[OVER + which * 32 + jnp.minimum(at, 31)]
                k, c = item // 4, item % 4
                apart = lax.bitwise_xor(group, k // 4)
                dyhi, dz, r2 = apart // Z, apart % Z, k % 2
                extra = bias[jnp.where(at < count, jnp.clip(table[CNT + k] - c * 4, 0, 4), 0)]
                store_partial(spare + j, queries_of(dyhi, dz, r2), tiles_of(k, c * 4), extra)
                units.append(unit_of(dyhi, dz, r2))
            for j in range(4):
                merge(units[j], [spare + j])
            return 0

        lax.fori_loop(0, (count + 3) // 4, four, 0)

    def resident():
        for r2 in range(2):
            r = 2 * half + r2
            here = jnp.clip(table[SCAL + 3 + r] - ctx * 512, 0, 512)
            q = queries_of(0, 0, r2)
            for c in range(8):
                limit = jnp.where(lane < (here - c * 64) * 4, bias[4], NONE)
                store_partial(spare + r2 * 8 + c, q, cache[r, c * 256 : (c + 1) * 256, :], limit)
        for r2 in range(2):
            merge(unit_of(0, 0, r2), [spare + r2 * 8 + c for c in range(8)])

    def finish(dyhi):
        row, lane = iota((128, 128), 0) % 32, iota((128, 128), 1)
        for pair in range(Z // 2):
            total = jnp.zeros((4, 128), f32)
            for j in range(4):
                dz, r2 = 2 * pair + j // 2, j % 2
                u = unit_of(dyhi, dz, r2)
                l = st_l[u]
                o = (st_acc[u] / l).astype(bf16)
                lse = jnp.where(lane == row + 32 * j, st_m[u] + jnp.log2(l), 0.0)
                total = total + jnp.sum(lse.reshape(4, 32, 128), axis=1)
                for t, (i, rows) in enumerate(places(dyhi, dz, r2)):
                    outs[i][rows, :] = o[t * 32 : (t + 1) * 32]
            for t in range(4):
                if half:
                    kept[t // 2, pl.ds((2 * dyhi + t % 2) * 4 + pair, 1), :] = total[t : t + 1]
                else:
                    kept[0, pl.ds(t * 4 + pair, 1), :] = total[t : t + 1]

    def per_group_half(work):
        if half:
            lax.fori_loop(0, 2, lambda dyhi, _: (work(dyhi), 0)[1], 0)
        else:
            work(d // 2)

    per_group_half(first)
    if half:
        beyond(1)
        beyond(3)
        resident()
    else:
        beyond(lax.bitwise_xor(group // Z, d // 2) * 2)
        if d < 2:
            resident()
    per_group_half(finish)
    for i in range(n):
        for j, part in enumerate(split3(kept[i])):
            outs[i][2048 + 16 * j : 2064 + 16 * j, :] = part


def shares(lses):
    top = functools.reduce(jnp.maximum, lses)
    parts = [jnp.exp2(l - top) for l in lses]
    total = functools.reduce(jnp.add, parts)
    return [p / total for p in parts], top + jnp.log2(total)


def mixed(weights, tiles):
    eye = iota((128, 128), 0) == iota((128, 128), 1)
    scales = jnp.concatenate([jnp.where(eye, w, 0.0).astype(bf16) for w in weights], axis=1)
    return jnp.dot(scales, jnp.concatenate(tiles, axis=0), preferred_element_type=f32)


def lse_of(ref, n):
    tail = ref[128 * n :, :].astype(f32)
    return tail[0:n] + tail[n : 2 * n] + tail[2 * n : 3 * n]


def put_lse(ref, lse):
    n = lse.shape[0]
    rows = [p.astype(f32) for p in split3(lse)]
    rows.append(jnp.zeros((16 - 3 * n, 128), f32))
    ref[128 * n :, :] = jnp.concatenate(rows, axis=0).astype(bf16)


def merged(ins, n):
    weights, lse = shares([lse_of(ref, n) for ref in ins])
    outs = []
    for p in range(n):
        o = mixed([w[p : p + 1] for w in weights], [ref[p * 128 : (p + 1) * 128, :] for ref in ins])
        outs.append(o.astype(bf16))
    return outs, lse


def put(outs, tiles, lse):
    n = len(tiles) // len(outs)
    for i, out in enumerate(outs):
        for j in range(n):
            out[j * 128 : (j + 1) * 128, :] = tiles[i * n + j]
        put_lse(out, lse[i * n : (i + 1) * n])


def plane_kernel(*refs):
    put(refs[4:8], *merged(refs[:4], 16))


def line_kernel(*refs):
    left = iota((4, 128), 1) < 64
    (a, lse_a), (b, lse_b) = merged(refs[:4], 4), merged(refs[4:8], 4)

    def turned(lse):
        return pltpu.roll(jnp.concatenate([lse, lse], axis=0), 64, 1)[0:4]

    even = jnp.where(left, lse_a, turned(lse_b))
    odd = jnp.where(left, turned(lse_a), lse_b)
    tiles, rows = [], []
    for p in range(4):
        for i, lse in ((0, even), (1, odd)):
            half = slice(64 * i, 64 * i + 64)
            tiles.append(jnp.concatenate([a[p][half], b[p][half]], axis=0))
            rows.append(lse[p : p + 1])
    order = (0, 4, 2, 6, 1, 5, 3, 7)
    put(refs[8:10], [tiles[i] for i in order], jnp.concatenate([rows[i] for i in order], axis=0))


def halve_kernel(n, one, two, low, high):
    put((low, high), *merged((one, two), n))


def last_kernel(one, two, o_fresh, lse_fresh, out):
    weights, _ = shares([lse_of(one, 1), lse_of(two, 1), lse_fresh[0:1, :]])
    out[...] = mixed(weights, [one[0:128, :], two[0:128, :], o_fresh[...]]).astype(bf16)


def call(kernel, outs, ins, scratch=(), specs=None, out_specs=None, flops=0, size=0):
    shapes = [jax.ShapeDtypeStruct(s, d) for s, d in outs]
    return pl.pallas_call(
        kernel,
        out_shape=shapes,
        in_specs=specs or [VMEM] * len(ins),
        out_specs=out_specs or [VMEM] * len(outs),
        scratch_shapes=list(scratch),
        compiler_params=pltpu.CompilerParams(vmem_limit_bytes=40 << 20),
        cost_estimate=pl.CostEstimate(flops=flops, bytes_accessed=size, transcendentals=0),
    )(*ins)


def body(queries, fresh_key_value, key_value_cache, lens, blocks, block_group, block_request):
    ctx, grp, head = (lax.axis_index(a) for a in ("ctx", "grp", "head"))
    pair = [(0, 1), (1, 0)]
    tie = lax.optimization_barrier
    q = queries.reshape(4, 16, 2, 128).transpose(0, 2, 1, 3).reshape(2, 1, 1, 1, 64, 128)
    scal = jnp.concatenate([jnp.stack([grp, ctx, head]).astype(jnp.int32), lens[0]])
    key = block_group[:, 0] * 4 + block_request

    q, blocks, key_value_cache, key = tie((q, blocks, key_value_cache, key))
    line = jnp.concatenate([q, swapped(q, dz=4)], axis=1)
    mine, other = call(
        split_kernel,
        [((64, 64, 256), bf16)] * 2,
        [scal, blocks.reshape(64, 128, 256)],
        specs=[SMEM, VMEM],
        flops=1 << 30,
        size=8 << 20,
    )
    line, mine, other, key_value_cache, key = tie((line, mine, other, key_value_cache, key))
    line = jnp.concatenate([line, swapped(line, dz=2)], axis=2)
    theirs = lax.ppermute(other, "head", pair)
    keys = jnp.concatenate([key, lax.ppermute(key, "head", pair)], axis=0)
    line, keys, key_value_cache, q = tie((line, keys, key_value_cache, q))
    line = jnp.concatenate([line, swapped(line, dz=1)], axis=3)
    line, key_value_cache, theirs = tie((line, key_value_cache, theirs))
    line_a, line_b = line[0].reshape(512, 128), line[1].reshape(512, 128)
    plane_b = jnp.concatenate([line_b] + [swapped(line_b, dy=d) for d in (1, 2, 3)], axis=0)
    plane_a = jnp.concatenate([line_a] + [swapped(line_a, dx=d) for d in (1, 2, 3)], axis=0)
    rows = key_value_cache.reshape(4, 512, 4, 2, 128).transpose(0, 1, 3, 2, 4).reshape(16384, 128)
    (cache,) = call(cache_kernel, [((8192, 256), bf16)], [rows], size=8 << 20)
    cache = cache.reshape(4, 2048, 256)
    plane_a, plane_b, keys, mine, theirs = tie((plane_a, plane_b, keys, mine, theirs))
    qa, qb = {0: plane_a}, {0: plane_b}
    for d in (1, 3):
        qb[d] = swapped(plane_b, dx=d)
    for d in (1, 3):
        qa[d] = swapped(plane_a, dy=d)
    (table,) = call(
        index_kernel, [((TABLE,), jnp.int32)], [scal, keys], specs=[SMEM] * 2, out_specs=[SMEM], flops=4 << 30
    )
    blk = jnp.concatenate([mine, theirs], axis=0)
    o_fresh, lse_fresh = call(
        fresh_kernel, [((128, 128), bf16), ((8, 128), f32)], [q.reshape(128, 128), fresh_key_value.reshape(64, 256)]
    )
    plane_b, qb[1], qb[3] = tie((plane_b, qb[1], qb[3]))
    qb[2] = swapped(plane_b, dx=2)
    plane_a, qa[1], qa[3] = tie((plane_a, qa[1], qa[3]))
    qa[2] = swapped(plane_a, dy=2)

    def piece(half, d, q_in, table):
        n = 1 + half
        return call(
            functools.partial(piece_kernel, half, d),
            [((2096, 128), bf16)] * n,
            [table, *q_in, blk, cache],
            scratch=[pltpu.VMEM((5, 8, 256), f32)]
            + [pltpu.VMEM((16 * n + 16, 128, 128), f32)] * 3
            + [pltpu.VMEM((n, 16, 128), f32)],
            specs=[SMEM] + [VMEM] * (n + 2),
            flops=8 << 28,
            size=10 << 20,
        )

    pa, pb = {}, {}
    for half, d in ((0, 0), (1, 1), (0, 1), (0, 3), (0, 2), (1, 0)):
        if half:
            one, two = (1, 3) if d else (0, 2)
            if not d:
                pb[1], pb[3], table = tie((pb[1], pb[3], table))
            pb[one], pb[two] = piece(1, d, [qb[one], qb[two]], table)
            pb[one], pb[two], table = tie((pb[one], pb[two], table))
            for i in (one, two):
                pb[i] = swapped(pb[i], dx=i) if i else pb[i]
        else:
            (pa[d],) = piece(0, d, [qa[d]], table)
            pa[d], table = tie((pa[d], table))
            pa[d] = swapped(pa[d], dy=d) if d else pa[d]
    planes = [((528, 128), bf16)] * 4
    ca = call(plane_kernel, planes, [pa[d] for d in range(4)], size=3 << 20)
    cb = call(plane_kernel, planes, [pb[d] for d in range(4)], size=3 << 20)
    ca = [ca[0]] + [swapped(ca[d], dx=d) for d in (1, 2, 3)]
    cb = [cb[0]] + [swapped(cb[d], dy=d) for d in (1, 2, 3)]
    low, high = call(line_kernel, [((528, 128), bf16)] * 2, [*ca, *cb], size=2 << 20)
    low, high = call(functools.partial(halve_kernel, 4), [((272, 128), bf16)] * 2, [low, swapped(high, dz=1)])
    low, high = call(functools.partial(halve_kernel, 2), [((144, 128), bf16)] * 2, [low, swapped(high, dz=2)])
    (out,) = call(last_kernel, [((128, 128), bf16)], [low, swapped(high, dz=4), o_fresh, lse_fresh])
    return out.reshape(4, 2, 16, 128).transpose(0, 2, 1, 3).reshape(queries.shape)


def solution(mesh):
    return jax.shard_map(
        body,
        mesh=mesh,
        in_specs=(
            P("grp", None, None, "head", "ctx"),
            P("grp", None, None, "head", None),
            P("grp", None, "ctx", "head", None),
            P("grp", None),
            P(("ctx", "grp", "head"), None, None, None),
            P(("ctx", "grp", "head"), None),
            P(("ctx", "grp", "head")),
        ),
        out_specs=P("grp", None, None, "head", "ctx"),
        check_vma=False,
    )
```

```python
import functools

import jax
import jax.numpy as jnp
from jax import lax
from jax.experimental import pallas as pl
from jax.experimental.pallas import tpu as pltpu
from jax.sharding import PartitionSpec as P

NONE = -1e30
X, Y, Z = 4, 4, 8
LOG2E = 1.4426950408889634
CNT, OVER, NOVER, SCAL, TABLE = 1024, 1088, 1216, 1220, 1280
VMEM = pl.BlockSpec(memory_space=pltpu.VMEM)
SMEM = pl.BlockSpec(memory_space=pltpu.SMEM)
bf16, f32 = jnp.bfloat16, jnp.float32


def place(x, y, z):
    return ((y % 2) * X + x) * (2 * Z) + (y // 2) * Z + z


def swapped(value, dx=0, dy=0, dz=0):
    route = [
        (place(x, y, z), place(x ^ dx, y ^ dy, z ^ dz))
        for x in range(X)
        for y in range(Y)
        for z in range(Z)
    ]
    return lax.ppermute(value, ("ctx", "grp"), route)


def iota(shape, dim):
    return lax.broadcasted_iota(jnp.int32, shape, dim)


def split3(value):
    high = value.astype(bf16)
    rest = value - high.astype(f32)
    middle = rest.astype(bf16)
    low = (rest - middle.astype(f32)).astype(bf16)
    return high, middle, low


def scores(q, k):
    return lax.dot_general(q, k, (((1,), (1,)), ((), ())), preferred_element_type=f32)


def fresh_kernel(q_ref, kv_ref, o_ref, lse_ref):
    s = scores(q_ref[...], kv_ref[:, :128]) * (128**-0.5 * LOG2E)
    row, col = iota(s.shape, 0), iota(s.shape, 1)
    valid = (row // 32 == col // 16) & (row % 4 == col % 4) & ((col % 16) // 4 <= (row % 16) // 4)
    s = jnp.where(valid, s, NONE)
    m = jnp.max(s, axis=1, keepdims=True)
    p = jnp.exp2(s - m)
    l = jnp.sum(p, axis=1, keepdims=True)
    acc = jnp.dot(p.astype(bf16), kv_ref[:, 128:], preferred_element_type=f32)
    o_ref[...] = (acc / l).astype(bf16)
    lse = jnp.broadcast_to(m + jnp.log2(l), (128, 128))
    eye = iota((128, 128), 0) == iota((128, 128), 1)
    lse_ref[...] = jnp.broadcast_to(jnp.sum(jnp.where(eye, lse, 0.0), axis=0, keepdims=True), (8, 128))


def split_kernel(scal, blocks, mine, other):
    row, lane = iota((128, 128), 0), iota((128, 128), 1)
    first = 4 * scal[2]
    start = jnp.where(row < 64, first, 4 - first)
    at = row % 64
    select = jnp.where(lane == (at // 4) * 8 + start + at % 4, 1.0, 0.0).astype(bf16)

    def eight(i, _):
        for j in range(8):
            b = i * 8 + j
            both = jnp.dot(select, blocks[b], preferred_element_type=f32).astype(bf16)
            mine[b] = both[:64]
            other[b] = both[64:]
        return 0

    lax.fori_loop(0, 8, eight, 0)


def cache_kernel(mixed_rows, cache):
    row, lane = iota((128, 128), 0), iota((128, 128), 1)
    at = row % 64
    select = jnp.where(lane == (at // 4) * 8 + (row // 64) * 4 + at % 4, 1.0, 0.0).astype(bf16)

    def sixteen(i, _):
        for j in range(16):
            b = i * 16 + j
            here = mixed_rows[pl.ds(pl.multiple_of(b * 128, 128), 128), :]
            both = jnp.dot(select, here, preferred_element_type=f32).astype(bf16)
            rows = pl.ds(pl.multiple_of(b * 64, 64), 64)
            cache[rows, :128] = both[:64]
            cache[rows, 128:] = both[64:]
        return 0

    lax.fori_loop(0, 8, sixteen, 0)


def index_kernel(scal, keys, table):
    for i in range(7):
        table[SCAL + i] = scal[i]

    def clear(i, _):
        table[CNT + i] = 0
        for j in range(16):
            table[i * 16 + j] = 0
        table[OVER + 2 * i] = 0
        table[OVER + 2 * i + 1] = 0
        return 0

    lax.fori_loop(0, 64, clear, 0)
    for i in range(4):
        table[NOVER + i] = 0

    def enter(i, _):
        k = keys[i]
        c = table[CNT + k]
        table[k * 16 + jnp.minimum(c, 15)] = i
        table[CNT + k] = c + 1

        @pl.when((c % 4 == 0) & (c > 0) & (c < 16))
        def _():
            which = (k // 32) * 2 + (k % 4) // 2
            n = table[NOVER + which]
            table[OVER + which * 32 + jnp.minimum(n, 31)] = k * 4 + c // 4
            table[NOVER + which] = n + 1

        return 0

    lax.fori_loop(0, 128, enter, 0)


def piece_kernel(half, d, table, *refs):
    n = 1 + half
    q_refs, (blk, cache), outs = refs[:n], refs[n : n + 2], refs[n + 2 : 2 * n + 2]
    bias, st_m, st_l, st_acc, kept = refs[2 * n + 2 :]
    scale = 128**-0.5 * LOG2E
    group, ctx = table[SCAL], table[SCAL + 1]
    row, lane = iota((8, 256), 0), iota((8, 256), 1)
    for i in range(5):
        bias[i] = jnp.where((row % 4 == lane % 4) & (lane < i * 64), 0.0, NONE)
    ones = jnp.ones((256, 128), bf16)
    unit_count = 16 * n
    spare = unit_count

    def places(dyhi, dz, r2):
        if half:
            slots = [(i, (2 * dyhi + dylo) * Z + dz) for i in range(2) for dylo in range(2)]
        else:
            slots = [(0, dx * Z + dz) for dx in range(X)]
        return [(i, pl.ds(pl.multiple_of(s * 64 + r2 * 32, 32), 32)) for i, s in slots]

    def queries_of(dyhi, dz, r2):
        return jnp.concatenate([q_refs[i][rows, :] for i, rows in places(dyhi, dz, r2)], axis=0)

    def unit_of(dyhi, dz, r2):
        return (dyhi * Z + dz) * 2 + r2 if half else dz * 2 + r2

    def tiles_of(k, start):
        return jnp.concatenate([blk[table[k * 16 + start + j]] for j in range(4)], axis=0)

    def store_partial(u, q, kv, extra):
        s = scores(q, kv[:, :128])
        s = (s.reshape(16, 8, 256) * scale + extra[None]).reshape(128, 256)
        m = jnp.max(s, axis=1, keepdims=True)
        p = jnp.exp2(s - m).astype(bf16)
        both = jnp.dot(p, jnp.concatenate([ones, kv[:, 128:]], axis=1), preferred_element_type=f32)
        st_m[u] = jnp.broadcast_to(m, (128, 128))
        st_l[u] = both[:, :128]
        st_acc[u] = both[:, 128:]

    def merge(u, others):
        ms = [st_m[i] for i in [u, *others]]
        top = functools.reduce(jnp.maximum, ms)
        ws = [jnp.exp2(m - top) for m in ms]
        l = functools.reduce(jnp.add, [w * st_l[i] for w, i in zip(ws, [u, *others])])
        acc = functools.reduce(jnp.add, [w * st_acc[i] for w, i in zip(ws, [u, *others])])
        st_m[u] = top
        st_l[u] = l
        st_acc[u] = acc

    def first(dyhi):
        for dz in range(Z):
            for r2 in range(2):
                k = lax.bitwise_xor(group, dyhi * Z + dz) * 4 + 2 * half + r2
                extra = bias[jnp.minimum(table[CNT + k], 4)]
                store_partial(unit_of(dyhi, dz, r2), queries_of(dyhi, dz, r2), tiles_of(k, 0), extra)

    def beyond(which):
        count = table[NOVER + which]

        def four(i, _):
            units = []
            for j in range(4):
                at = i * 4 + j
                item = table[OVER + which * 32 + jnp.minimum(at, 31)]
                k, c = item // 4, item % 4
                apart = lax.bitwise_xor(group, k // 4)
                dyhi, dz, r2 = apart // Z, apart % Z, k % 2
                extra = bias[jnp.where(at < count, jnp.clip(table[CNT + k] - c * 4, 0, 4), 0)]
                store_partial(spare + j, queries_of(dyhi, dz, r2), tiles_of(k, c * 4), extra)
                units.append(unit_of(dyhi, dz, r2))
            for j in range(4):
                merge(units[j], [spare + j])
            return 0

        lax.fori_loop(0, (count + 3) // 4, four, 0)

    def resident():
        for r2 in range(2):
            r = 2 * half + r2
            here = jnp.clip(table[SCAL + 3 + r] - ctx * 512, 0, 512)
            q = queries_of(0, 0, r2)
            for c in range(8):
                limit = jnp.where(lane < (here - c * 64) * 4, bias[4], NONE)
                store_partial(spare + r2 * 8 + c, q, cache[r, c * 256 : (c + 1) * 256, :], limit)
        for r2 in range(2):
            merge(unit_of(0, 0, r2), [spare + r2 * 8 + c for c in range(8)])

    def finish(dyhi):
        row, lane = iota((128, 128), 0) % 32, iota((128, 128), 1)
        for pair in range(Z // 2):
            total = jnp.zeros((4, 128), f32)
            for j in range(4):
                dz, r2 = 2 * pair + j // 2, j % 2
                u = unit_of(dyhi, dz, r2)
                l = st_l[u]
                o = (st_acc[u] / l).astype(bf16)
                lse = jnp.where(lane == row + 32 * j, st_m[u] + jnp.log2(l), 0.0)
                total = total + jnp.sum(lse.reshape(4, 32, 128), axis=1)
                for t, (i, rows) in enumerate(places(dyhi, dz, r2)):
                    outs[i][rows, :] = o[t * 32 : (t + 1) * 32]
            for t in range(4):
                if half:
                    kept[t // 2, pl.ds((2 * dyhi + t % 2) * 4 + pair, 1), :] = total[t : t + 1]
                else:
                    kept[0, pl.ds(t * 4 + pair, 1), :] = total[t : t + 1]

    def per_group_half(work):
        if half:
            lax.fori_loop(0, 2, lambda dyhi, _: (work(dyhi), 0)[1], 0)
        else:
            work(d // 2)

    per_group_half(first)
    if half:
        beyond(1)
        beyond(3)
        resident()
    else:
        beyond(lax.bitwise_xor(group // Z, d // 2) * 2)
        if d < 2:
            resident()
    per_group_half(finish)
    for i in range(n):
        for j, part in enumerate(split3(kept[i])):
            outs[i][2048 + 16 * j : 2064 + 16 * j, :] = part


def shares(lses):
    top = functools.reduce(jnp.maximum, lses)
    parts = [jnp.exp2(l - top) for l in lses]
    total = functools.reduce(jnp.add, parts)
    return [p / total for p in parts], top + jnp.log2(total)


def mixed(weights, tiles):
    eye = iota((128, 128), 0) == iota((128, 128), 1)
    scales = jnp.concatenate([jnp.where(eye, w, 0.0).astype(bf16) for w in weights], axis=1)
    return jnp.dot(scales, jnp.concatenate(tiles, axis=0), preferred_element_type=f32)


def lse_of(ref, n):
    tail = ref[128 * n :, :].astype(f32)
    return tail[0:n] + tail[n : 2 * n] + tail[2 * n : 3 * n]


def put_lse(ref, lse):
    n = lse.shape[0]
    rows = [p.astype(f32) for p in split3(lse)]
    rows.append(jnp.zeros((16 - 3 * n, 128), f32))
    ref[128 * n :, :] = jnp.concatenate(rows, axis=0).astype(bf16)


def merged(ins, n):
    weights, lse = shares([lse_of(ref, n) for ref in ins])
    outs = []
    for p in range(n):
        o = mixed([w[p : p + 1] for w in weights], [ref[p * 128 : (p + 1) * 128, :] for ref in ins])
        outs.append(o.astype(bf16))
    return outs, lse


def put(outs, tiles, lse):
    n = len(tiles) // len(outs)
    for i, out in enumerate(outs):
        for j in range(n):
            out[j * 128 : (j + 1) * 128, :] = tiles[i * n + j]
        put_lse(out, lse[i * n : (i + 1) * n])


def plane_kernel(*refs):
    put(refs[4:8], *merged(refs[:4], 16))


def line_kernel(*refs):
    left = iota((4, 128), 1) < 64
    (a, lse_a), (b, lse_b) = merged(refs[:4], 4), merged(refs[4:8], 4)

    def turned(lse):
        return pltpu.roll(jnp.concatenate([lse, lse], axis=0), 64, 1)[0:4]

    even = jnp.where(left, lse_a, turned(lse_b))
    odd = jnp.where(left, turned(lse_a), lse_b)
    tiles, rows = [], []
    for p in range(4):
        for i, lse in ((0, even), (1, odd)):
            half = slice(64 * i, 64 * i + 64)
            tiles.append(jnp.concatenate([a[p][half], b[p][half]], axis=0))
            rows.append(lse[p : p + 1])
    order = (0, 4, 2, 6, 1, 5, 3, 7)
    put(refs[8:10], [tiles[i] for i in order], jnp.concatenate([rows[i] for i in order], axis=0))


def halve_kernel(n, one, two, low, high):
    put((low, high), *merged((one, two), n))


def last_kernel(one, two, o_fresh, lse_fresh, out):
    weights, _ = shares([lse_of(one, 1), lse_of(two, 1), lse_fresh[0:1, :]])
    out[...] = mixed(weights, [one[0:128, :], two[0:128, :], o_fresh[...]]).astype(bf16)


def call(kernel, outs, ins, scratch=(), specs=None, out_specs=None, flops=0, size=0):
    shapes = [jax.ShapeDtypeStruct(s, d) for s, d in outs]
    return pl.pallas_call(
        kernel,
        out_shape=shapes,
        in_specs=specs or [VMEM] * len(ins),
        out_specs=out_specs or [VMEM] * len(outs),
        scratch_shapes=list(scratch),
        compiler_params=pltpu.CompilerParams(vmem_limit_bytes=40 << 20),
        cost_estimate=pl.CostEstimate(flops=flops, bytes_accessed=size, transcendentals=0),
    )(*ins)


def body(queries, fresh_key_value, key_value_cache, lens, blocks, block_group, block_request):
    ctx, grp, head = (lax.axis_index(a) for a in ("ctx", "grp", "head"))
    pair = [(0, 1), (1, 0)]
    tie = lax.optimization_barrier
    q = queries.reshape(4, 16, 2, 128).transpose(0, 2, 1, 3).reshape(2, 1, 1, 1, 64, 128)
    scal = jnp.concatenate([jnp.stack([grp, ctx, head]).astype(jnp.int32), lens[0]])
    key = block_group[:, 0] * 4 + block_request

    q, blocks, key_value_cache, key = tie((q, blocks, key_value_cache, key))
    line = jnp.concatenate([q, swapped(q, dz=4)], axis=1)
    mine, other = call(
        split_kernel,
        [((64, 64, 256), bf16)] * 2,
        [scal, blocks.reshape(64, 128, 256)],
        specs=[SMEM, VMEM],
        flops=1 << 30,
        size=8 << 20,
    )
    line, mine, other, key_value_cache, key = tie((line, mine, other, key_value_cache, key))
    line = jnp.concatenate([line, swapped(line, dz=2)], axis=2)
    theirs = lax.ppermute(other, "head", pair)
    keys = jnp.concatenate([key, lax.ppermute(key, "head", pair)], axis=0)
    line, keys, key_value_cache, q = tie((line, keys, key_value_cache, q))
    line = jnp.concatenate([line, swapped(line, dz=1)], axis=3)
    line, key_value_cache, theirs = tie((line, key_value_cache, theirs))
    line_a, line_b = line[0].reshape(512, 128), line[1].reshape(512, 128)
    plane_b = jnp.concatenate([line_b] + [swapped(line_b, dy=d) for d in (1, 2, 3)], axis=0)
    plane_a = jnp.concatenate([line_a] + [swapped(line_a, dx=d) for d in (1, 2, 3)], axis=0)
    rows = key_value_cache.reshape(4, 512, 4, 2, 128).transpose(0, 1, 3, 2, 4).reshape(16384, 128)
    (cache,) = call(cache_kernel, [((8192, 256), bf16)], [rows], size=8 << 20)
    cache = cache.reshape(4, 2048, 256)
    plane_b, keys, mine, theirs = tie((plane_b, keys, mine, theirs))
    qa, qb = {0: plane_a}, {0: plane_b}
    for d in (1, 3):
        qb[d] = swapped(plane_b, dx=d)
    for d in (1, 3):
        qa[d] = swapped(plane_a, dy=d)
    (table,) = call(
        index_kernel, [((TABLE,), jnp.int32)], [scal, keys], specs=[SMEM] * 2, out_specs=[SMEM], flops=4 << 30
    )
    blk = jnp.concatenate([mine, theirs], axis=0)
    o_fresh, lse_fresh = call(
        fresh_kernel, [((128, 128), bf16), ((8, 128), f32)], [q.reshape(128, 128), fresh_key_value.reshape(64, 256)]
    )
    plane_b, qb[1], qb[3] = tie((plane_b, qb[1], qb[3]))
    qb[2] = swapped(plane_b, dx=2)
    plane_a, qa[1], qa[3] = tie((plane_a, qa[1], qa[3]))
    qa[2] = swapped(plane_a, dy=2)

    def piece(half, d, q_in, table):
        n = 1 + half
        return call(
            functools.partial(piece_kernel, half, d),
            [((2096, 128), bf16)] * n,
            [table, *q_in, blk, cache],
            scratch=[pltpu.VMEM((5, 8, 256), f32)]
            + [pltpu.VMEM((16 * n + 16, 128, 128), f32)] * 3
            + [pltpu.VMEM((n, 16, 128), f32)],
            specs=[SMEM] + [VMEM] * (n + 2),
            flops=8 << 28,
            size=10 << 20,
        )

    pa, pb = {}, {}
    for half, d in ((0, 0), (1, 1), (0, 1), (0, 3), (0, 2), (1, 0)):
        if half:
            one, two = (1, 3) if d else (0, 2)
            if not d:
                pb[1], pb[3], table = tie((pb[1], pb[3], table))
            pb[one], pb[two] = piece(1, d, [qb[one], qb[two]], table)
            pb[one], pb[two], table = tie((pb[one], pb[two], table))
            for i in (one, two):
                pb[i] = swapped(pb[i], dx=i) if i else pb[i]
        else:
            (pa[d],) = piece(0, d, [qa[d]], table)
            pa[d], table = tie((pa[d], table))
            pa[d] = swapped(pa[d], dy=d) if d else pa[d]
    planes = [((528, 128), bf16)] * 4
    ca = call(plane_kernel, planes, [pa[d] for d in range(4)], size=3 << 20)
    cb = call(plane_kernel, planes, [pb[d] for d in range(4)], size=3 << 20)
    ca = [ca[0]] + [swapped(ca[d], dx=d) for d in (1, 2, 3)]
    cb = [cb[0]] + [swapped(cb[d], dy=d) for d in (1, 2, 3)]
    low, high = call(line_kernel, [((528, 128), bf16)] * 2, [*ca, *cb], size=2 << 20)
    low, high = call(functools.partial(halve_kernel, 4), [((272, 128), bf16)] * 2, [low, swapped(high, dz=1)])
    low, high = call(functools.partial(halve_kernel, 2), [((144, 128), bf16)] * 2, [low, swapped(high, dz=2)])
    (out,) = call(last_kernel, [((128, 128), bf16)], [low, swapped(high, dz=4), o_fresh, lse_fresh])
    return out.reshape(4, 2, 16, 128).transpose(0, 2, 1, 3).reshape(queries.shape)


def solution(mesh):
    return jax.shard_map(
        body,
        mesh=mesh,
        in_specs=(
            P("grp", None, None, "head", "ctx"),
            P("grp", None, None, "head", None),
            P("grp", None, "ctx", "head", None),
            P("grp", None),
            P(("ctx", "grp", "head"), None, None, None),
            P(("ctx", "grp", "head"), None),
            P(("ctx", "grp", "head")),
        ),
        out_specs=P("grp", None, None, "head", "ctx"),
        check_vma=False,
    )
```
